256 devices in a mesh: roll: 8 (over z), pipe: 2 (over core), tp: 16 (over y, x).
Axes of the slice: x: 4, y: 4, z: 8, core: 2. Of those that a mesh axis runs over, the one named last changes fastest.
Arguments:
- ssm_state: bfloat16 [2, 128, 128, 64, 128], P('pipe', 'roll', 'tp'), may hold values from -6 to 6
- conv_window: bfloat16 [2, 128, 3, 8192], P('pipe', 'roll', None, 'tp'), may hold values from -6 to 6
- x_in: bfloat16 [4, 128, 8192], P(None, 'roll', 'tp'), may hold values from -6 to 6
- z_gate: bfloat16 [2, 4, 128, 8192], P('pipe', None, 'roll', 'tp'), may hold values from -6 to 6
- dt_raw: float32 [2, 4, 128, 128], P('pipe', None, 'roll', 'tp'), may hold values from -3 to 3
- b_in: bfloat16 [2, 4, 128, 128], P('pipe', None, 'roll'), may hold values from -6 to 6
- c_in: bfloat16 [2, 4, 128, 128], P('pipe', None, 'roll'), may hold values from -0.5 to 0.5
- conv_weight: bfloat16 [2, 4, 8192], P('pipe', None, 'tp'), may hold values from -3 to 3
- a_log: float32 [2, 128], P('pipe', 'tp'), may hold values from 0 to 2.8
- dt_bias: float32 [2, 128], P('pipe', 'tp'), may hold values from -4 to -1
- skip_d: float32 [2, 128], P('pipe', 'tp'), may hold values from 0.5 to 1.5
- norm_gain: float32 [2, 8192], P('pipe', 'tp'), may hold values from 0.5 to 1.5
- parent: int32 [128], replicated, may hold values from 0 to 127, as said below
Outputs:
- layer_out: bfloat16 [2, 4, 128, 8192], P('pipe', None, 'roll', 'tp')
The draws below stay inside these ranges and needn't reach their ends.
Inputs may be any that keep to these rules, and one draw needn't show every extreme that they name: Slot s's parent lies in the same aligned block of 16 slots as s or in the block just before; every block but the first has exactly 1 slot whose parent lies in the block before, the first has none.
All inputs are finite; a program needn't handle non-finite values.
Results may differ from the reference program's by a relative error of at most 0.003.
Values may be sent and summed in bfloat16 or wider, within the bound.
No kernel may reach another device: no remote copies, remote signals or barrier semaphores. Data moves between devices by JAX's collectives and lax.ppermute only.
A program may use at most 64 MiB of HBM per device.

```python
import jax
import jax.numpy as jnp
from jax import lax

HEADS = 128
HEAD_DIM = 64
STATE = 128
CONV = 4
STEPS = 4
CROSS = 1
SEQ_DEV = 16
SEQS = 128


def draw_parent(key, part):
    key = jax.random.fold_in(key, 7)
    blocks = SEQS // SEQ_DEV
    key_rank, key_own, key_prev = jax.random.split(key, 3)
    scores = jax.random.randint(key_rank, (blocks, SEQ_DEV), 0, 1 << 20) * SEQ_DEV + jnp.arange(SEQ_DEV, dtype=jnp.int32)[None, :]
    order = jnp.argsort(jnp.argsort(scores, axis=1, stable=True), axis=1, stable=True)
    block_ids = jnp.arange(blocks, dtype=jnp.int32)[:, None]
    crossing = (order < CROSS) & (block_ids >= 1)
    own_pick = jax.random.randint(key_own, (blocks, SEQ_DEV), 0, SEQ_DEV)
    prev_pick = jax.random.randint(key_prev, (blocks, SEQ_DEV), 0, SEQ_DEV)
    parent_ids = jnp.where(crossing, (block_ids - 1) * SEQ_DEV + prev_pick, block_ids * SEQ_DEV + own_pick)
    return parent_ids.reshape(SEQS).astype(jnp.int32)


def block_scale(key, dims, shards, smallest, top_value):
    def one(dim, shards_of):
        draws = jax.random.uniform(jax.random.fold_in(jax.random.fold_in(key, 6), dim), (shards_of,), jnp.float32, smallest / len(shards), top_value / len(shards))
        return jnp.repeat(jnp.exp(draws), dims[dim] // shards_of).reshape((-1,) + (1,) * (len(dims) - dim - 1))

    loudness = one(*shards[0])
    for cut in shards[1:]:
        loudness = loudness * one(*cut)
    return loudness


def bell_draw(key, extent, deviation, limit, pieces=(), kind=jnp.bfloat16):
    drawn = deviation * jax.random.normal(key, extent, jnp.float32)
    if pieces:
        drawn = drawn * block_scale(key, extent, pieces, -0.22, 0.18)
    return jnp.clip(drawn, -limit, limit).astype(kind)


def setup_inputs(seed: int = 0) -> dict:
    arg_keys = jax.random.split(jax.random.key(seed), 14)
    return {
        "ssm_state": bell_draw(arg_keys[0], (2, SEQS, HEADS, HEAD_DIM, STATE), 1.0, 6.0, ((0, 2), (1, 8), (2, 16))),
        "conv_window": bell_draw(arg_keys[1], (2, SEQS, CONV - 1, HEADS * HEAD_DIM), 1.0, 6.0, ((0, 2), (1, 8), (3, 16))),
        "x_in": bell_draw(arg_keys[2], (STEPS, SEQS, HEADS * HEAD_DIM), 1.0, 6.0, ((1, 8), (2, 16))),
        "z_gate": bell_draw(arg_keys[3], (2, STEPS, SEQS, HEADS * HEAD_DIM), 1.0, 6.0, ((0, 2), (2, 8), (3, 16))),
        "dt_raw": bell_draw(arg_keys[4], (2, STEPS, SEQS, HEADS), 0.5, 3.0, ((0, 2), (2, 8), (3, 16)), jnp.float32),
        "b_in": bell_draw(arg_keys[5], (2, STEPS, SEQS, STATE), 1.0, 6.0, ((0, 2), (2, 8))),
        "c_in": bell_draw(arg_keys[6], (2, STEPS, SEQS, STATE), STATE ** -0.5, 0.5, ((0, 2), (2, 8))),
        "conv_weight": bell_draw(arg_keys[7], (2, CONV, HEADS * HEAD_DIM), CONV ** -0.5, 3.0, ((0, 2), (2, 16))),
        "a_log": jnp.clip(2.8 * jax.random.uniform(arg_keys[8], (2, HEADS), jnp.float32) ** block_scale(arg_keys[8], (2, HEADS), ((0, 2), (1, 16)), -0.2, 0.2), 0.0, 2.8),
        "dt_bias": jnp.clip(-4.0 + 3.0 * jax.random.uniform(arg_keys[9], (2, HEADS), jnp.float32) ** block_scale(arg_keys[9], (2, HEADS), ((0, 2), (1, 16)), -0.2, 0.2), -4.0, -1.0),
        "skip_d": jnp.clip(0.5 + 1.0 * jax.random.uniform(arg_keys[10], (2, HEADS), jnp.float32) ** block_scale(arg_keys[10], (2, HEADS), ((0, 2), (1, 16)), -0.2, 0.2), 0.5, 1.5),
        "norm_gain": jnp.clip(1.0 + 0.1 * jax.random.normal(arg_keys[11], (2, HEADS * HEAD_DIM), jnp.float32), 0.5, 1.5),
        "parent": draw_parent(jax.random.fold_in(arg_keys[13], 71), 0),
    }


def layer_steps(state, window, inputs, z_rows, dt_rows, b_rows, c_rows, taps, a_log, dt_bias, skip_d, gain):
    hstate = state.astype(jnp.float32)
    outputs = []
    for step in range(STEPS):
        x_row = inputs[step]
        stacked = jnp.concatenate([window, x_row[None]], axis=0).astype(jnp.float32)
        xc = jax.nn.silu(lax.optimization_barrier(jnp.sum(stacked * taps.astype(jnp.float32), axis=0)))
        delta = jax.nn.softplus(dt_rows[step] + dt_bias)
        decay = jnp.exp(-delta * jnp.exp(a_log))
        x_heads = xc.reshape(HEADS, HEAD_DIM)
        b_row = b_rows[step].astype(jnp.float32)
        c_row = c_rows[step].astype(jnp.float32)
        hstate = decay[:, None, None] * hstate + (delta[:, None] * x_heads)[:, :, None] * b_row[None, None, :]
        y_heads = jnp.einsum('hpn,n->hp', hstate, c_row, precision=lax.Precision.HIGHEST) + skip_d[:, None] * x_heads
        gated = y_heads.reshape(-1) * jax.nn.silu(z_rows[step].astype(jnp.float32))
        scale = lax.rsqrt(jnp.mean(gated * gated) + 1e-05)
        outputs.append((gated * scale * gain).astype(jnp.bfloat16))
        window = jnp.concatenate([window[1:], x_row[None]], axis=0)
    return jnp.stack(outputs)

def reference(ssm_state, conv_window, x_in, z_gate, dt_raw, b_in, c_in, conv_weight, a_log, dt_bias, skip_d, norm_gain, parent):

    def one_slot(slot):
        source = parent[slot]
        inputs = x_in[:, slot]
        results = []
        for layer in range(2):
            inputs = layer_steps(ssm_state[layer, source], conv_window[layer, source], inputs, z_gate[layer, :, slot], dt_raw[layer, :, slot], b_in[layer, :, slot], c_in[layer, :, slot], conv_weight[layer], a_log[layer], dt_bias[layer], skip_d[layer], norm_gain[layer])
            results.append(inputs)
        return jnp.stack(results)
    mapped = lax.map(one_slot, jnp.arange(SEQS, dtype=jnp.int32))
    return jnp.transpose(mapped, (1, 2, 0, 3))
```

```python
import jax
import jax.numpy as jnp
from jax import lax
from jax.experimental import pallas as pl
from jax.experimental.pallas import tpu as pltpu
from jax.sharding import PartitionSpec as P

F32 = jnp.float32
BF16 = jnp.bfloat16
VMEM = pl.BlockSpec(memory_space=pltpu.VMEM)
SMEM = pl.BlockSpec(memory_space=pltpu.SMEM)
ANY = pl.BlockSpec(memory_space=pl.ANY)
NT = (((1,), (1,)), ((), ()))
EPS = 1e-05
PARAMS = pltpu.CompilerParams(vmem_limit_bytes=24 * 1024 * 1024)


def silu(value):
    return value / (1.0 + jnp.exp(-value))


def pairs(steps):
    return [(t, r) for t in range(steps) for r in range(t + 1)]


def crossing_kernel(parent, state, window, out, sem):
    slots = window.shape[1]
    nrows = state.shape[1]
    count = lax.axis_size("roll")
    following = lax.rem(lax.axis_index("roll") + 1, count)
    begin = following * slots

    def look(s, found):
        row = parent[begin + s] - begin + slots
        return jnp.where(row < slots, row, found)

    row = lax.fori_loop(0, slots, look, jnp.int32(0), unroll=True)
    row = jnp.clip(row, 0, slots - 1)
    copy = pltpu.make_async_copy(state.at[row], out.at[pl.ds(0, nrows)], sem)
    copy.start()
    taps, _, width = window.shape
    groups = width // 128
    pick = lax.broadcasted_iota(jnp.int32, (slots, 1), 0) == row
    place = lax.broadcasted_iota(jnp.int32, (out.shape[0] - nrows, 128), 0)
    packed = jnp.zeros(place.shape, F32)
    for k in range(taps):
        chosen = jnp.sum(jnp.where(pick, window[k].astype(F32), 0.0), axis=0, keepdims=True)
        for j in range(groups):
            packed = jnp.where(place == k * groups + j, chosen[:, j * 128:(j + 1) * 128], packed)
    out[pl.ds(nrows, place.shape[0])] = packed.astype(BF16)
    copy.wait()


def local_kernel(
    parent, state, window, c_in, b_in, dt_raw, z_gate, conv, a_log, dt_bias, skip_d,
    base_out, reach_out, mix_out, conv_out, cmask_out, wmask_out,
    held, sems,
):
    steps, slots, width = z_gate.shape
    heads = dt_raw.shape[1]
    taps = window.shape[0]
    nstate = c_in.shape[2]
    first = lax.axis_index("roll") * slots
    local = []
    copies = []
    for s in range(slots):
        row = parent[first + s] - first
        local.append(row)
        copy = pltpu.make_async_copy(state.at[jnp.clip(row, 0, slots - 1)], held.at[s], sems.at[s])
        copy.start()
        copies.append(copy)

    slot_col = lax.broadcasted_iota(jnp.int32, (slots, slots), 0)
    slot_row = lax.broadcasted_iota(jnp.int32, (slots, slots), 1)
    choose = jnp.zeros((slots, slots), F32)
    slot_lane = lax.broadcasted_iota(jnp.int32, (slots, 128), 0)
    inside = jnp.zeros((slots, 128), F32)
    for s in range(slots):
        choose = jnp.where((slot_col == s) & (slot_row == local[s]), 1.0, choose)
        inside = jnp.where((slot_lane == s) & (local[s] >= 0), 1.0, inside)
    outside = 1.0 - inside
    wmask_out[...] = outside
    choose = choose.astype(BF16)

    taken = [jnp.dot(choose, window[k], preferred_element_type=F32) for k in range(taps)]
    weight = [conv[pl.ds(k, 1), :].astype(F32) for k in range(taps + 1)]
    for t in range(taps):
        part = weight[0] * taken[t]
        for k in range(1, taps - t):
            part = part + weight[k] * taken[t + k]
        conv_out[t] = part

    rate = jnp.exp(a_log[...])
    delta, decay = [], []
    for t in range(steps):
        raw = jnp.transpose(dt_raw[t]) + dt_bias[...]
        delta.append(jnp.maximum(raw, 0.0) + jnp.log1p(jnp.exp(-jnp.abs(raw))))
        decay.append(jnp.exp(-delta[t] * rate))
    c_rows = [c_in[t].astype(F32) for t in range(steps)]
    b_rows = [b_in[t].astype(F32) for t in range(steps)]
    coefs = []
    running = None
    for t in range(steps):
        running = decay[t] if running is None else running * decay[t]
        coefs.append(running)
    for t, r in pairs(steps):
        dot = jnp.sum(c_rows[t] * b_rows[r], axis=1, keepdims=True)
        coef = delta[r] * dot
        for j in range(r + 1, t + 1):
            coef = coef * decay[j]
        if t == r:
            coef = coef + skip_d[...]
        coefs.append(coef)
    stacked = jnp.concatenate(coefs, axis=0)
    head = lax.broadcasted_iota(jnp.int32, (heads, width), 0)
    lane_head = lax.broadcasted_iota(jnp.int32, (heads, width), 1) // (width // heads)
    expand = jnp.where(head == lane_head, 1.0, 0.0).astype(BF16)
    high = stacked.astype(BF16)
    low = (stacked - high.astype(F32)).astype(BF16)
    spread = jnp.dot(high, expand, preferred_element_type=F32) + jnp.dot(low, expand, preferred_element_type=F32)
    gate = [silu(z_gate[t].astype(F32)) for t in range(steps)]
    reach = []
    for t in range(steps):
        reach.append(spread[t * slots:(t + 1) * slots] * gate[t])
        reach_out[t] = reach[t]
    for i, (t, _) in enumerate(pairs(steps)):
        mix_out[i] = spread[(steps + i) * slots:(steps + i + 1) * slots] * gate[t]

    c_all = jnp.concatenate(c_rows, axis=0)
    slot_of = lax.rem(lax.broadcasted_iota(jnp.int32, (steps * slots, nstate), 0), slots)
    all_outside = jnp.concatenate([outside] * steps, axis=0)
    all_inside = 1.0 - all_outside
    cmask_out[...] = (c_all * all_outside).astype(BF16)
    c_inside = c_all * all_inside
    total = None
    for s in range(0, slots, 2):
        copies[s].wait()
        copies[s + 1].wait()
        lhs = jnp.concatenate(
            [jnp.where(slot_of == s + i, c_inside, 0.0).astype(BF16) for i in range(2)], axis=1
        )
        rhs = jnp.concatenate([held[s], held[s + 1]], axis=1)
        part = lax.dot_general(lhs, rhs, NT, preferred_element_type=F32)
        total = part if total is None else total + part
    for t in range(steps):
        base_out[t] = total[t * slots:(t + 1) * slots] * reach[t]


def gated_rows(pre, base, mix, steps):
    inner = [silu(value) for value in pre]
    rows = list(base)
    for i, (t, r) in enumerate(pairs(steps)):
        rows[t] = rows[t] + mix[i] * inner[r]
    return rows


def square_sums(rows):
    squares = []
    for row in rows:
        sq = row * row
        part = sq[:, :128]
        for j in range(1, sq.shape[1] // 128):
            part = part + sq[:, j * 128:(j + 1) * 128]
        squares.append(part)
    flat = jnp.concatenate(squares, axis=0)
    flat = jnp.concatenate([flat, jnp.zeros((128 - flat.shape[0], 128), F32)], axis=0)
    return jnp.sum(jnp.transpose(flat), axis=0, keepdims=True)


def row_scales(parts, channels, rows):
    totals = jnp.sum(parts, axis=0)[:1]
    scale = lax.rsqrt(totals * (1.0 / channels) + EPS)
    return jnp.transpose(jnp.broadcast_to(scale, (128, 128)))[:rows]


def scaled(row, scale):
    return jnp.concatenate(
        [row[:, j * 128:(j + 1) * 128] * scale for j in range(row.shape[1] // 128)], axis=1
    )


def first_kernel(arrived, base, reach, mix, conv_part, cmask, wmask, conv, x_in, gain,
                 base_out, conv_out, send_out, sums_out):
    steps, slots, width = x_in.shape
    taps = conv_part.shape[0]
    nrows = arrived.shape[0] - 16
    groups = width // 128
    extra = lax.dot_general(cmask[...], arrived[pl.ds(0, nrows)], NT, preferred_element_type=F32)
    start = []
    for t in range(steps):
        start.append(base[t] + extra[t * slots:(t + 1) * slots] * reach[t])
        base_out[t] = start[t]
    packed = arrived[pl.ds(nrows, 16)].astype(F32)
    rows = [
        jnp.concatenate([packed[k * groups + j:k * groups + j + 1] for j in range(groups)], axis=1)
        for k in range(taps)
    ]
    weight = [conv[pl.ds(k, 1), :].astype(F32) for k in range(taps + 1)]
    mask = wmask[:, :1]
    pre = []
    for t in range(taps):
        part = weight[0] * rows[t]
        for k in range(1, taps - t):
            part = part + weight[k] * rows[t + k]
        pre.append(conv_part[t] + mask * part)
        conv_out[t] = pre[t]
    x_rows = [x_in[t].astype(F32) for t in range(steps)]
    pre = with_inputs(pre, weight, x_rows)
    gated = gated_rows(pre, start, [mix[i] for i in range(mix.shape[0])], steps)
    for t in range(steps):
        send_out[t] = gated[t] * gain[...]
    sums_out[...] = jnp.broadcast_to(square_sums(gated)[None], sums_out.shape)


def with_inputs(window_part, weight, x_rows):
    taps = len(window_part)
    pre = []
    for t in range(len(x_rows)):
        part = window_part[t] if t < taps else None
        for k in range(max(0, taps - t), taps + 1):
            term = weight[k] * x_rows[t + k - taps]
            part = term if part is None else part + term
        pre.append(part)
    return pre


def second_kernel(sums, own, other, base, mix, conv_part, conv, channels, norm_out, gated_out, sums_out):
    steps, slots, width = own.shape
    taps = conv_part.shape[0]
    scale = row_scales(sums[...], channels, steps * slots)
    first = lax.axis_index("pipe") == 0
    rows = []
    for t in range(steps):
        row = jnp.where(first, own[t], other[t])
        row = scaled(row, scale[t * slots:(t + 1) * slots]).astype(BF16)
        norm_out[t] = row
        rows.append(row.astype(F32))
    weight = [conv[pl.ds(k, 1), :].astype(F32) for k in range(taps + 1)]
    pre = with_inputs([conv_part[t] for t in range(taps)], weight, rows)
    gated = gated_rows(pre, [base[t] for t in range(steps)], [mix[i] for i in range(mix.shape[0])], steps)
    for t in range(steps):
        gated_out[t] = gated[t]
    sums_out[...] = jnp.broadcast_to(square_sums(gated)[None], sums_out.shape)


def last_kernel(sums, norm, gated, gain, channels, out):
    steps, slots, width = gated.shape
    scale = row_scales(sums[...], channels, steps * slots)
    first = lax.axis_index("pipe") == 0
    for t in range(steps):
        row = scaled(gated[t], scale[t * slots:(t + 1) * slots]) * gain[...]
        out[t] = jnp.where(first, norm[t].astype(F32), row).astype(BF16)


def body(ssm_state, conv_window, x_in, z_gate, dt_raw, b_in, c_in, conv_weight, a_log, dt_bias, skip_d, norm_gain, parent):
    _, slots, heads, head_dim, nstate = ssm_state.shape
    steps, _, width = x_in.shape
    taps = conv_window.shape[2]
    rows = heads * head_dim
    tp = lax.axis_size("tp")
    pipes = lax.axis_size("pipe")
    count = lax.axis_size("roll")
    channels = width * tp
    npairs = len(pairs(steps))
    state = ssm_state.reshape(slots, rows, nstate)
    window = jnp.transpose(conv_window[0], (1, 0, 2))
    raw = jnp.transpose(dt_raw[0], (0, 2, 1))
    shape = jax.ShapeDtypeStruct

    leaving = pl.pallas_call(
        crossing_kernel,
        out_shape=shape((rows + 16, nstate), BF16),
        in_specs=[SMEM, ANY, VMEM],
        out_specs=VMEM,
        scratch_shapes=[pltpu.SemaphoreType.DMA],
        compiler_params=PARAMS,
        name="crossing",
    )(parent, state, window)
    arrived = lax.ppermute(leaving, "roll", [(i, (i + 1) % count) for i in range(count)])

    base, reach, mix, conv_part, cmask, wmask = pl.pallas_call(
        local_kernel,
        out_shape=(
            shape((steps, slots, width), F32),
            shape((steps, slots, width), F32),
            shape((npairs, slots, width), F32),
            shape((taps, slots, width), F32),
            shape((steps * slots, nstate), BF16),
            shape((slots, 128), F32),
        ),
        in_specs=[SMEM, ANY] + [VMEM] * 9,
        out_specs=(VMEM,) * 6,
        scratch_shapes=[
            pltpu.VMEM((slots, rows, nstate), BF16),
            pltpu.SemaphoreType.DMA((slots,)),
        ],
        compiler_params=PARAMS,
        cost_estimate=pl.CostEstimate(flops=20_000_000, bytes_accessed=4_000_000, transcendentals=0),
        name="local",
    )(parent, state, window, c_in[0], b_in[0], raw, z_gate[0], conv_weight[0], a_log, dt_bias, skip_d)

    base, conv_part, own, sums = pl.pallas_call(
        first_kernel,
        out_shape=(
            shape((steps, slots, width), F32),
            shape((taps, slots, width), F32),
            shape((steps, slots, width), F32),
            shape((pipes * tp, 8, 128), F32),
        ),
        in_specs=[VMEM] * 10,
        out_specs=(VMEM,) * 4,
        compiler_params=PARAMS,
        name="first",
    )(arrived, base, reach, mix, conv_part, cmask, wmask, conv_weight[0], x_in, norm_gain)
    other = lax.ppermute(own, "pipe", [(i, (i + 1) % pipes) for i in range(pipes)])
    sums = lax.all_to_all(sums, ("pipe", "tp"), 0, 0)

    norm, gated, sums = pl.pallas_call(
        lambda sums, *refs: second_kernel(sums.at[pl.ds(0, tp)], *refs[:6], channels, *refs[6:]),
        out_shape=(
            shape((steps, slots, width), BF16),
            shape((steps, slots, width), F32),
            shape((tp, 8, 128), F32),
        ),
        in_specs=[VMEM] * 7,
        out_specs=(VMEM,) * 3,
        compiler_params=PARAMS,
        name="second",
    )(sums, own, other, base, mix, conv_part, conv_weight[0])
    sums = lax.all_to_all(sums, "tp", 0, 0)

    result = pl.pallas_call(
        lambda sums, norm, gated, gain, out: last_kernel(sums, norm, gated, gain, channels, out),
        out_shape=shape((steps, slots, width), BF16),
        in_specs=[VMEM] * 4,
        out_specs=VMEM,
        compiler_params=PARAMS,
        name="last",
    )(sums, norm, gated, norm_gain)
    return result[None]


def solution(mesh):
    in_specs = (
        P("pipe", "roll", "tp", None, None),
        P("pipe", "roll", None, "tp"),
        P(None, "roll", "tp"),
        P("pipe", None, "roll", "tp"),
        P("pipe", None, "roll", "tp"),
        P("pipe", None, "roll", None),
        P("pipe", None, "roll", None),
        P("pipe", None, "tp"),
        P("pipe", "tp"),
        P("pipe", "tp"),
        P("pipe", "tp"),
        P("pipe", "tp"),
        P(),
    )
    out_specs = P("pipe", None, "roll", "tp")
    return jax.shard_map(body, mesh=mesh, in_specs=in_specs, out_specs=out_specs, check_vma=False)
```

```python
import jax
import jax.numpy as jnp
from jax import lax
from jax.experimental import pallas as pl
from jax.experimental.pallas import tpu as pltpu
from jax.sharding import PartitionSpec as P

F32 = jnp.float32
BF16 = jnp.bfloat16
VMEM = pl.BlockSpec(memory_space=pltpu.VMEM)
SMEM = pl.BlockSpec(memory_space=pltpu.SMEM)
HBM = pl.BlockSpec(memory_space=pltpu.HBM)
NT = (((1,), (1,)), ((), ()))
EPS = 1e-05
PARAMS = pltpu.CompilerParams(vmem_limit_bytes=24 * 1024 * 1024)


def silu(value):
    return value / (1.0 + jnp.exp(-value))


def pairs(steps):
    return [(t, r) for t in range(steps) for r in range(t + 1)]


def crossing_kernel(parent_hbm, state, window_hbm, out, parent, window, sems):
    get_parent = pltpu.make_async_copy(parent_hbm, parent, sems.at[0])
    get_parent.start()
    get_window = pltpu.make_async_copy(window_hbm, window, sems.at[1])
    get_window.start()
    slots = window.shape[1]
    nrows = state.shape[1]
    count = lax.axis_size("roll")
    following = lax.rem(lax.axis_index("roll") + 1, count)
    begin = following * slots
    get_parent.wait()

    row = jnp.int32(0)
    for s in range(slots):
        found = parent[begin + s] - begin + slots
        row = jnp.where(found < slots, found, row)
    row = jnp.clip(row, 0, slots - 1)
    copy = pltpu.make_async_copy(state.at[row], out.at[pl.ds(0, nrows)], sems.at[2])
    copy.start()
    taps, _, width = window.shape
    groups = width // 128
    pick = lax.broadcasted_iota(jnp.int32, (slots, 1), 0) == row
    place = lax.broadcasted_iota(jnp.int32, (out.shape[0] - nrows, 128), 0)
    packed = jnp.zeros(place.shape, F32)
    get_window.wait()
    for k in range(taps):
        chosen = jnp.sum(jnp.where(pick, window[k].astype(F32), 0.0), axis=0, keepdims=True)
        for j in range(groups):
            packed = jnp.where(place == k * groups + j, chosen[:, j * 128:(j + 1) * 128], packed)
    out[pl.ds(nrows, place.shape[0])] = packed.astype(BF16)
    copy.wait()


def local_kernel(
    parent, state, window, c_in, b_in, dt_raw, z_gate, conv, a_log, dt_bias, skip_d,
    base_out, reach_out, mix_out, conv_out, cmask_out, wmask_out,
):
    steps, slots, width = z_gate.shape
    heads = dt_raw.shape[1]
    taps = window.shape[0]
    nstate = c_in.shape[2]
    first = lax.axis_index("roll") * slots
    local = [parent[first + s] - first for s in range(slots)]
    held = [jnp.clip(row, 0, slots - 1) for row in local]

    slot_col = lax.broadcasted_iota(jnp.int32, (slots, slots), 0)
    slot_row = lax.broadcasted_iota(jnp.int32, (slots, slots), 1)
    choose = jnp.zeros((slots, slots), F32)
    slot_lane = lax.broadcasted_iota(jnp.int32, (slots, 128), 0)
    inside = jnp.zeros((slots, 128), F32)
    for s in range(slots):
        choose = jnp.where((slot_col == s) & (slot_row == local[s]), 1.0, choose)
        inside = jnp.where((slot_lane == s) & (local[s] >= 0), 1.0, inside)
    outside = 1.0 - inside
    wmask_out[...] = outside
    choose = choose.astype(BF16)

    taken = [jnp.dot(choose, window[k], preferred_element_type=F32) for k in range(taps)]
    weight = [conv[pl.ds(k, 1), :].astype(F32) for k in range(taps + 1)]
    for t in range(taps):
        part = weight[0] * taken[t]
        for k in range(1, taps - t):
            part = part + weight[k] * taken[t + k]
        conv_out[t] = part

    rate = jnp.exp(a_log[...])
    delta, decay = [], []
    for t in range(steps):
        raw = jnp.transpose(dt_raw[t]) + dt_bias[...]
        delta.append(jnp.maximum(raw, 0.0) + jnp.log1p(jnp.exp(-jnp.abs(raw))))
        decay.append(jnp.exp(-delta[t] * rate))
    c_rows = [c_in[t].astype(F32) for t in range(steps)]
    b_rows = [b_in[t].astype(F32) for t in range(steps)]
    coefs = []
    running = None
    for t in range(steps):
        running = decay[t] if running is None else running * decay[t]
        coefs.append(running)
    for t, r in pairs(steps):
        dot = jnp.sum(c_rows[t] * b_rows[r], axis=1, keepdims=True)
        coef = delta[r] * dot
        for j in range(r + 1, t + 1):
            coef = coef * decay[j]
        if t == r:
            coef = coef + skip_d[...]
        coefs.append(coef)
    stacked = jnp.concatenate(coefs, axis=0)
    head = lax.broadcasted_iota(jnp.int32, (heads, width), 0)
    lane_head = lax.broadcasted_iota(jnp.int32, (heads, width), 1) // (width // heads)
    expand = jnp.where(head == lane_head, 1.0, 0.0).astype(BF16)
    high = stacked.astype(BF16)
    low = (stacked - high.astype(F32)).astype(BF16)
    spread = jnp.dot(high, expand, preferred_element_type=F32) + jnp.dot(low, expand, preferred_element_type=F32)
    gate = [silu(z_gate[t].astype(F32)) for t in range(steps)]
    reach = []
    for t in range(steps):
        reach.append(spread[t * slots:(t + 1) * slots] * gate[t])
        reach_out[t] = reach[t]
    for i, (t, _) in enumerate(pairs(steps)):
        mix_out[i] = spread[(steps + i) * slots:(steps + i + 1) * slots] * gate[t]

    c_all = jnp.concatenate(c_rows, axis=0)
    slot_of = lax.rem(lax.broadcasted_iota(jnp.int32, (steps * slots, nstate), 0), slots)
    all_outside = jnp.concatenate([outside] * steps, axis=0)
    all_inside = 1.0 - all_outside
    cmask_out[...] = (c_all * all_outside).astype(BF16)
    c_inside = c_all * all_inside
    total = None
    for s in range(0, slots, 2):
        lhs = jnp.concatenate(
            [jnp.where(slot_of == s + i, c_inside, 0.0).astype(BF16) for i in range(2)], axis=1
        )
        rhs = jnp.concatenate([state[held[s]], state[held[s + 1]]], axis=1)
        part = lax.dot_general(lhs, rhs, NT, preferred_element_type=F32)
        total = part if total is None else total + part
    for t in range(steps):
        base_out[t] = total[t * slots:(t + 1) * slots] * reach[t]


def gated_rows(pre, base, mix, steps):
    inner = [silu(value) for value in pre]
    rows = list(base)
    for i, (t, r) in enumerate(pairs(steps)):
        rows[t] = rows[t] + mix[i] * inner[r]
    return rows


def square_sums(rows):
    squares = []
    for row in rows:
        sq = row * row
        part = sq[:, :128]
        for j in range(1, sq.shape[1] // 128):
            part = part + sq[:, j * 128:(j + 1) * 128]
        squares.append(part)
    flat = jnp.concatenate(squares, axis=0)
    flat = jnp.concatenate([flat, jnp.zeros((128 - flat.shape[0], 128), F32)], axis=0)
    return jnp.sum(jnp.transpose(flat), axis=0, keepdims=True)


def row_scales(parts, channels, rows):
    totals = jnp.sum(parts, axis=0)[:1]
    scale = lax.rsqrt(totals * (1.0 / channels) + EPS)
    return jnp.transpose(jnp.broadcast_to(scale, (128, 128)))[:rows]


def scaled(row, scale):
    return jnp.concatenate(
        [row[:, j * 128:(j + 1) * 128] * scale for j in range(row.shape[1] // 128)], axis=1
    )


def first_kernel(arrived, base, reach, mix, conv_part, cmask, wmask, conv, x_in, gain,
                 base_out, conv_out, send_out, sums_out):
    steps, slots, width = x_in.shape
    taps = conv_part.shape[0]
    nrows = arrived.shape[0] - 16
    groups = width // 128
    extra = lax.dot_general(cmask[...], arrived[pl.ds(0, nrows)], NT, preferred_element_type=F32)
    start = []
    for t in range(steps):
        start.append(base[t] + extra[t * slots:(t + 1) * slots] * reach[t])
        base_out[t] = start[t]
    packed = arrived[pl.ds(nrows, 16)].astype(F32)
    rows = [
        jnp.concatenate([packed[k * groups + j:k * groups + j + 1] for j in range(groups)], axis=1)
        for k in range(taps)
    ]
    weight = [conv[pl.ds(k, 1), :].astype(F32) for k in range(taps + 1)]
    mask = wmask[:, :1]
    pre = []
    for t in range(taps):
        part = weight[0] * rows[t]
        for k in range(1, taps - t):
            part = part + weight[k] * rows[t + k]
        pre.append(conv_part[t] + mask * part)
        conv_out[t] = pre[t]
    x_rows = [x_in[t].astype(F32) for t in range(steps)]
    pre = with_inputs(pre, weight, x_rows)
    gated = gated_rows(pre, start, [mix[i] for i in range(mix.shape[0])], steps)
    for t in range(steps):
        send_out[t] = gated[t] * gain[...]
    sums_out[...] = jnp.broadcast_to(square_sums(gated)[None], sums_out.shape)


def with_inputs(window_part, weight, x_rows):
    taps = len(window_part)
    pre = []
    for t in range(len(x_rows)):
        part = window_part[t] if t < taps else None
        for k in range(max(0, taps - t), taps + 1):
            term = weight[k] * x_rows[t + k - taps]
            part = term if part is None else part + term
        pre.append(part)
    return pre


def second_kernel(sums, own, other, base, mix, conv_part, conv, channels, norm_out, gated_out, sums_out):
    steps, slots, width = own.shape
    taps = conv_part.shape[0]
    scale = row_scales(sums[...], channels, steps * slots)
    first = lax.axis_index("pipe") == 0
    rows = []
    for t in range(steps):
        row = jnp.where(first, own[t], other[t])
        row = scaled(row, scale[t * slots:(t + 1) * slots]).astype(BF16)
        norm_out[t] = row
        rows.append(row.astype(F32))
    weight = [conv[pl.ds(k, 1), :].astype(F32) for k in range(taps + 1)]
    pre = with_inputs([conv_part[t] for t in range(taps)], weight, rows)
    gated = gated_rows(pre, [base[t] for t in range(steps)], [mix[i] for i in range(mix.shape[0])], steps)
    for t in range(steps):
        gated_out[t] = gated[t]
    sums_out[...] = jnp.broadcast_to(square_sums(gated)[None], sums_out.shape)


def last_kernel(sums, norm, gated, gain, channels, out):
    steps, slots, width = gated.shape
    scale = row_scales(sums[...], channels, steps * slots)
    first = lax.axis_index("pipe") == 0
    for t in range(steps):
        row = scaled(gated[t], scale[t * slots:(t + 1) * slots]) * gain[...]
        out[t] = jnp.where(first, norm[t].astype(F32), row).astype(BF16)


def body(ssm_state, conv_window, x_in, z_gate, dt_raw, b_in, c_in, conv_weight, a_log, dt_bias, skip_d, norm_gain, parent):
    _, slots, heads, head_dim, nstate = ssm_state.shape
    steps, _, width = x_in.shape
    taps = conv_window.shape[2]
    rows = heads * head_dim
    tp = lax.axis_size("tp")
    pipes = lax.axis_size("pipe")
    count = lax.axis_size("roll")
    channels = width * tp
    npairs = len(pairs(steps))
    state = ssm_state.reshape(slots, rows, nstate)
    window = jnp.transpose(conv_window[0], (1, 0, 2))
    raw = jnp.transpose(dt_raw[0], (0, 2, 1))
    shape = jax.ShapeDtypeStruct

    leaving = pl.pallas_call(
        crossing_kernel,
        out_shape=shape((rows + 16, nstate), BF16),
        in_specs=[HBM, HBM, HBM],
        out_specs=VMEM,
        scratch_shapes=[
            pltpu.SMEM(parent.shape, jnp.int32),
            pltpu.VMEM(window.shape, BF16),
            pltpu.SemaphoreType.DMA((3,)),
        ],
        compiler_params=PARAMS,
        name="crossing",
    )(*[pltpu.with_memory_space_constraint(value, pltpu.HBM) for value in (parent, state, window)])
    arrived = lax.ppermute(leaving, "roll", [(i, (i + 1) % count) for i in range(count)])

    base, reach, mix, conv_part, cmask, wmask = pl.pallas_call(
        local_kernel,
        out_shape=(
            shape((steps, slots, width), F32),
            shape((steps, slots, width), F32),
            shape((npairs, slots, width), F32),
            shape((taps, slots, width), F32),
            shape((steps * slots, nstate), BF16),
            shape((slots, 128), F32),
        ),
        in_specs=[SMEM] + [VMEM] * 10,
        out_specs=(VMEM,) * 6,
        compiler_params=PARAMS,
        cost_estimate=pl.CostEstimate(flops=20_000_000, bytes_accessed=4_000_000, transcendentals=0),
        name="local",
    )(parent, state, window, c_in[0], b_in[0], raw, z_gate[0], conv_weight[0], a_log, dt_bias, skip_d)

    base, conv_part, own, sums = pl.pallas_call(
        first_kernel,
        out_shape=(
            shape((steps, slots, width), F32),
            shape((taps, slots, width), F32),
            shape((steps, slots, width), F32),
            shape((pipes * tp, 8, 128), F32),
        ),
        in_specs=[VMEM] * 10,
        out_specs=(VMEM,) * 4,
        compiler_params=PARAMS,
        name="first",
    )(arrived, base, reach, mix, conv_part, cmask, wmask, conv_weight[0], x_in, norm_gain)
    other = lax.ppermute(own, "pipe", [(i, (i + 1) % pipes) for i in range(pipes)])
    sums = lax.all_to_all(sums, ("pipe", "tp"), 0, 0)

    norm, gated, sums = pl.pallas_call(
        lambda sums, *refs: second_kernel(sums.at[pl.ds(0, tp)], *refs[:6], channels, *refs[6:]),
        out_shape=(
            shape((steps, slots, width), BF16),
            shape((steps, slots, width), F32),
            shape((tp, 8, 128), F32),
        ),
        in_specs=[VMEM] * 7,
        out_specs=(VMEM,) * 3,
        compiler_params=PARAMS,
        name="second",
    )(sums, own, other, base, mix, conv_part, conv_weight[0])
    sums = lax.all_to_all(sums, "tp", 0, 0)

    result = pl.pallas_call(
        lambda sums, norm, gated, gain, out: last_kernel(sums, norm, gated, gain, channels, out),
        out_shape=shape((steps, slots, width), BF16),
        in_specs=[VMEM] * 4,
        out_specs=VMEM,
        compiler_params=PARAMS,
        name="last",
    )(sums, norm, gated, norm_gain)
    return result[None]


def solution(mesh):
    in_specs = (
        P("pipe", "roll", "tp", None, None),
        P("pipe", "roll", None, "tp"),
        P(None, "roll", "tp"),
        P("pipe", None, "roll", "tp"),
        P("pipe", None, "roll", "tp"),
        P("pipe", None, "roll", None),
        P("pipe", None, "roll", None),
        P("pipe", None, "tp"),
        P("pipe", "tp"),
        P("pipe", "tp"),
        P("pipe", "tp"),
        P("pipe", "tp"),
        P(),
    )
    out_specs = P("pipe", None, "roll", "tp")
    return jax.shard_map(body, mesh=mesh, in_specs=in_specs, out_specs=out_specs, check_vma=False)
```

```python
import jax
import jax.numpy as jnp
from jax import lax
from jax.experimental import pallas as pl
from jax.experimental.pallas import tpu as pltpu
from jax.sharding import PartitionSpec as P

F32 = jnp.float32
BF16 = jnp.bfloat16
VMEM = pl.BlockSpec(memory_space=pltpu.VMEM)
SMEM = pl.BlockSpec(memory_space=pltpu.SMEM)
HBM = pl.BlockSpec(memory_space=pltpu.HBM)
NT = (((1,), (1,)), ((), ()))
EPS = 1e-05
PARAMS = pltpu.CompilerParams(vmem_limit_bytes=24 * 1024 * 1024)


def silu(value):
    return value / (1.0 + jnp.exp(-value))


def pairs(steps):
    return [(t, r) for t in range(steps) for r in range(t + 1)]


def crossing_kernel(parent_hbm, state, window_hbm, out, parent, window, sems):
    slots = window.shape[1]
    nrows = state.shape[1]
    taps, _, width = window.shape
    groups = width // 128
    following = lax.axis_index("roll") + 1

    @pl.when(following == lax.axis_size("roll"))
    def _():
        out[...] = jnp.zeros(out.shape, BF16)

    @pl.when(following < lax.axis_size("roll"))
    def _():
        get_parent = pltpu.make_async_copy(parent_hbm, parent, sems.at[0])
        get_parent.start()
        get_window = pltpu.make_async_copy(window_hbm, window, sems.at[1])
        get_window.start()
        begin = following * slots
        get_parent.wait()
        row = jnp.int32(0)
        for s in range(slots):
            found = parent[begin + s] - begin + slots
            row = jnp.where(found < slots, found, row)
        row = jnp.clip(row, 0, slots - 1)
        copy = pltpu.make_async_copy(state.at[row], out.at[pl.ds(0, nrows)], sems.at[2])
        copy.start()
        pick = lax.broadcasted_iota(jnp.int32, (slots, 1), 0) == row
        place = lax.broadcasted_iota(jnp.int32, (out.shape[0] - nrows, 128), 0)
        packed = jnp.zeros(place.shape, F32)
        get_window.wait()
        for k in range(taps):
            chosen = jnp.sum(jnp.where(pick, window[k].astype(F32), 0.0), axis=0, keepdims=True)
            for j in range(groups):
                packed = jnp.where(place == k * groups + j, chosen[:, j * 128:(j + 1) * 128], packed)
        out[pl.ds(nrows, place.shape[0])] = packed.astype(BF16)
        copy.wait()


def local_kernel(
    parent, state, window, c_in, b_in, dt_raw, z_gate, conv, a_log, dt_bias, skip_d,
    base_out, reach_out, mix_out, conv_out, cmask_out, wmask_out,
):
    steps, slots, width = z_gate.shape
    heads = dt_raw.shape[1]
    taps = window.shape[0]
    nstate = c_in.shape[2]
    first = lax.axis_index("roll") * slots
    local = [parent[first + s] - first for s in range(slots)]
    held = [jnp.clip(row, 0, slots - 1) for row in local]

    slot_col = lax.broadcasted_iota(jnp.int32, (slots, slots), 0)
    slot_row = lax.broadcasted_iota(jnp.int32, (slots, slots), 1)
    choose = jnp.zeros((slots, slots), F32)
    slot_lane = lax.broadcasted_iota(jnp.int32, (slots, 128), 0)
    inside = jnp.zeros((slots, 128), F32)
    for s in range(slots):
        choose = jnp.where((slot_col == s) & (slot_row == local[s]), 1.0, choose)
        inside = jnp.where((slot_lane == s) & (local[s] >= 0), 1.0, inside)
    outside = 1.0 - inside
    wmask_out[...] = outside
    choose = choose.astype(BF16)

    taken = [jnp.dot(choose, window[k], preferred_element_type=F32) for k in range(taps)]
    weight = [conv[pl.ds(k, 1), :].astype(F32) for k in range(taps + 1)]
    for t in range(taps):
        part = weight[0] * taken[t]
        for k in range(1, taps - t):
            part = part + weight[k] * taken[t + k]
        conv_out[t] = part

    rate = jnp.exp(a_log[...])
    delta, decay = [], []
    for t in range(steps):
        raw = jnp.transpose(dt_raw[t]) + dt_bias[...]
        delta.append(jnp.maximum(raw, 0.0) + jnp.log1p(jnp.exp(-jnp.abs(raw))))
        decay.append(jnp.exp(-delta[t] * rate))
    c_rows = [c_in[t].astype(F32) for t in range(steps)]
    b_rows = [b_in[t].astype(F32) for t in range(steps)]
    coefs = []
    running = None
    for t in range(steps):
        running = decay[t] if running is None else running * decay[t]
        coefs.append(running)
    for t, r in pairs(steps):
        dot = jnp.sum(c_rows[t] * b_rows[r], axis=1, keepdims=True)
        coef = delta[r] * dot
        for j in range(r + 1, t + 1):
            coef = coef * decay[j]
        if t == r:
            coef = coef + skip_d[...]
        coefs.append(coef)
    stacked = jnp.concatenate(coefs, axis=0)
    head = lax.broadcasted_iota(jnp.int32, (heads, width), 0)
    lane_head = lax.broadcasted_iota(jnp.int32, (heads, width), 1) // (width // heads)
    expand = jnp.where(head == lane_head, 1.0, 0.0).astype(BF16)
    high = stacked.astype(BF16)
    low = (stacked - high.astype(F32)).astype(BF16)
    spread = jnp.dot(high, expand, preferred_element_type=F32) + jnp.dot(low, expand, preferred_element_type=F32)
    gate = [silu(z_gate[t].astype(F32)) for t in range(steps)]
    reach = []
    for t in range(steps):
        reach.append(spread[t * slots:(t + 1) * slots] * gate[t])
        reach_out[t] = reach[t]
    for i, (t, _) in enumerate(pairs(steps)):
        mix_out[i] = spread[(steps + i) * slots:(steps + i + 1) * slots] * gate[t]

    c_all = jnp.concatenate(c_rows, axis=0)
    slot_of = lax.rem(lax.broadcasted_iota(jnp.int32, (steps * slots, nstate), 0), slots)
    all_outside = jnp.concatenate([outside] * steps, axis=0)
    all_inside = 1.0 - all_outside
    cmask_out[...] = (c_all * all_outside).astype(BF16)
    c_inside = c_all * all_inside
    total = None
    for s in range(0, slots, 2):
        lhs = jnp.concatenate(
            [jnp.where(slot_of == s + i, c_inside, 0.0).astype(BF16) for i in range(2)], axis=1
        )
        rhs = jnp.concatenate([state[held[s]], state[held[s + 1]]], axis=1)
        part = lax.dot_general(lhs, rhs, NT, preferred_element_type=F32)
        total = part if total is None else total + part
    for t in range(steps):
        base_out[t] = total[t * slots:(t + 1) * slots] * reach[t]


def gated_rows(pre, base, mix, steps):
    inner = [silu(value) for value in pre]
    rows = list(base)
    for i, (t, r) in enumerate(pairs(steps)):
        rows[t] = rows[t] + mix[i] * inner[r]
    return rows


def square_sums(rows):
    squares = []
    for row in rows:
        sq = row * row
        part = sq[:, :128]
        for j in range(1, sq.shape[1] // 128):
            part = part + sq[:, j * 128:(j + 1) * 128]
        squares.append(part)
    flat = jnp.concatenate(squares, axis=0)
    flat = jnp.concatenate([flat, jnp.zeros((128 - flat.shape[0], 128), F32)], axis=0)
    return jnp.sum(jnp.transpose(flat), axis=0, keepdims=True)


def row_scales(parts, channels, rows):
    totals = jnp.sum(parts, axis=0)[:1]
    scale = lax.rsqrt(totals * (1.0 / channels) + EPS)
    return jnp.transpose(jnp.broadcast_to(scale, (128, 128)))[:rows]


def scaled(row, scale):
    return jnp.concatenate(
        [row[:, j * 128:(j + 1) * 128] * scale for j in range(row.shape[1] // 128)], axis=1
    )


def first_kernel(arrived, base, reach, mix, conv_part, cmask, wmask, conv, x_in, gain,
                 base_out, conv_out, send_out, sums_out):
    steps, slots, width = x_in.shape
    taps = conv_part.shape[0]
    nrows = arrived.shape[0] - 16
    groups = width // 128
    extra = lax.dot_general(cmask[...], arrived[pl.ds(0, nrows)], NT, preferred_element_type=F32)
    start = []
    for t in range(steps):
        start.append(base[t] + extra[t * slots:(t + 1) * slots] * reach[t])
        base_out[t] = start[t]
    packed = arrived[pl.ds(nrows, 16)].astype(F32)
    rows = [
        jnp.concatenate([packed[k * groups + j:k * groups + j + 1] for j in range(groups)], axis=1)
        for k in range(taps)
    ]
    weight = [conv[pl.ds(k, 1), :].astype(F32) for k in range(taps + 1)]
    mask = wmask[:, :1]
    pre = []
    for t in range(taps):
        part = weight[0] * rows[t]
        for k in range(1, taps - t):
            part = part + weight[k] * rows[t + k]
        pre.append(conv_part[t] + mask * part)
        conv_out[t] = pre[t]
    x_rows = [x_in[t].astype(F32) for t in range(steps)]
    pre = with_inputs(pre, weight, x_rows)
    gated = gated_rows(pre, start, [mix[i] for i in range(mix.shape[0])], steps)
    for t in range(steps):
        send_out[t] = gated[t] * gain[...]
    sums_out[...] = jnp.broadcast_to(square_sums(gated)[None], sums_out.shape)


def with_inputs(window_part, weight, x_rows):
    taps = len(window_part)
    pre = []
    for t in range(len(x_rows)):
        part = window_part[t] if t < taps else None
        for k in range(max(0, taps - t), taps + 1):
            term = weight[k] * x_rows[t + k - taps]
            part = term if part is None else part + term
        pre.append(part)
    return pre


def second_kernel(sums, own, other, base, mix, conv_part, conv, channels, norm_out, gated_out, sums_out):
    steps, slots, width = own.shape
    taps = conv_part.shape[0]
    scale = row_scales(sums[...], channels, steps * slots)
    first = lax.axis_index("pipe") == 0
    rows = []
    for t in range(steps):
        row = jnp.where(first, own[t], other[t])
        row = scaled(row, scale[t * slots:(t + 1) * slots]).astype(BF16)
        norm_out[t] = row
        rows.append(row.astype(F32))
    weight = [conv[pl.ds(k, 1), :].astype(F32) for k in range(taps + 1)]
    pre = with_inputs([conv_part[t] for t in range(taps)], weight, rows)
    gated = gated_rows(pre, [base[t] for t in range(steps)], [mix[i] for i in range(mix.shape[0])], steps)
    for t in range(steps):
        gated_out[t] = gated[t]
    sums_out[...] = jnp.broadcast_to(square_sums(gated)[None], sums_out.shape)


def last_kernel(sums, norm, gated, gain, channels, out):
    steps, slots, width = gated.shape
    scale = row_scales(sums[...], channels, steps * slots)
    first = lax.axis_index("pipe") == 0
    for t in range(steps):
        row = scaled(gated[t], scale[t * slots:(t + 1) * slots]) * gain[...]
        out[t] = jnp.where(first, norm[t].astype(F32), row).astype(BF16)


def body(ssm_state, conv_window, x_in, z_gate, dt_raw, b_in, c_in, conv_weight, a_log, dt_bias, skip_d, norm_gain, parent):
    _, slots, heads, head_dim, nstate = ssm_state.shape
    steps, _, width = x_in.shape
    taps = conv_window.shape[2]
    rows = heads * head_dim
    tp = lax.axis_size("tp")
    pipes = lax.axis_size("pipe")
    count = lax.axis_size("roll")
    channels = width * tp
    npairs = len(pairs(steps))
    state = ssm_state.reshape(slots, rows, nstate)
    window = jnp.transpose(conv_window[0], (1, 0, 2))
    raw = jnp.transpose(dt_raw[0], (0, 2, 1))
    shape = jax.ShapeDtypeStruct

    leaving = pl.pallas_call(
        crossing_kernel,
        out_shape=shape((rows + 16, nstate), BF16),
        in_specs=[HBM, HBM, HBM],
        out_specs=VMEM,
        scratch_shapes=[
            pltpu.SMEM(parent.shape, jnp.int32),
            pltpu.VMEM(window.shape, BF16),
            pltpu.SemaphoreType.DMA((3,)),
        ],
        compiler_params=PARAMS,
        name="crossing",
    )(*[pltpu.with_memory_space_constraint(value, pltpu.HBM) for value in (parent, state, window)])
    arrived = lax.ppermute(leaving, "roll", [(i, (i + 1) % count) for i in range(count)])

    base, reach, mix, conv_part, cmask, wmask = pl.pallas_call(
        local_kernel,
        out_shape=(
            shape((steps, slots, width), F32),
            shape((steps, slots, width), F32),
            shape((npairs, slots, width), F32),
            shape((taps, slots, width), F32),
            shape((steps * slots, nstate), BF16),
            shape((slots, 128), F32),
        ),
        in_specs=[SMEM] + [VMEM] * 10,
        out_specs=(VMEM,) * 6,
        compiler_params=PARAMS,
        cost_estimate=pl.CostEstimate(flops=20_000_000, bytes_accessed=4_000_000, transcendentals=0),
        name="local",
    )(parent, state, window, c_in[0], b_in[0], raw, z_gate[0], conv_weight[0], a_log, dt_bias, skip_d)

    base, conv_part, own, sums = pl.pallas_call(
        first_kernel,
        out_shape=(
            shape((steps, slots, width), F32),
            shape((taps, slots, width), F32),
            shape((steps, slots, width), F32),
            shape((pipes * tp, 8, 128), F32),
        ),
        in_specs=[VMEM] * 10,
        out_specs=(VMEM,) * 4,
        compiler_params=PARAMS,
        name="first",
    )(arrived, base, reach, mix, conv_part, cmask, wmask, conv_weight[0], x_in, norm_gain)
    other = lax.ppermute(own, "pipe", [(i, (i + 1) % pipes) for i in range(pipes)])
    sums = lax.all_to_all(sums, ("pipe", "tp"), 0, 0)

    norm, gated, sums = pl.pallas_call(
        lambda sums, *refs: second_kernel(sums.at[pl.ds(0, tp)], *refs[:6], channels, *refs[6:]),
        out_shape=(
            shape((steps, slots, width), BF16),
            shape((steps, slots, width), F32),
            shape((tp, 8, 128), F32),
        ),
        in_specs=[VMEM] * 7,
        out_specs=(VMEM,) * 3,
        compiler_params=PARAMS,
        name="second",
    )(sums, own, other, base, mix, conv_part, conv_weight[0])
    sums = lax.all_to_all(sums, "tp", 0, 0)

    result = pl.pallas_call(
        lambda sums, norm, gated, gain, out: last_kernel(sums, norm, gated, gain, channels, out),
        out_shape=shape((steps, slots, width), BF16),
        in_specs=[VMEM] * 4,
        out_specs=VMEM,
        compiler_params=PARAMS,
        name="last",
    )(sums, norm, gated, norm_gain)
    return result[None]


def solution(mesh):
    in_specs = (
        P("pipe", "roll", "tp", None, None),
        P("pipe", "roll", None, "tp"),
        P(None, "roll", "tp"),
        P("pipe", None, "roll", "tp"),
        P("pipe", None, "roll", "tp"),
        P("pipe", None, "roll", None),
        P("pipe", None, "roll", None),
        P("pipe", None, "tp"),
        P("pipe", "tp"),
        P("pipe", "tp"),
        P("pipe", "tp"),
        P("pipe", "tp"),
        P(),
    )
    out_specs = P("pipe", None, "roll", "tp")
    return jax.shard_map(body, mesh=mesh, in_specs=in_specs, out_specs=out_specs, check_vma=False)
```

```python
import jax
import jax.numpy as jnp
from jax import lax
from jax.experimental import pallas as pl
from jax.experimental.pallas import tpu as pltpu
from jax.sharding import PartitionSpec as P

F32 = jnp.float32
BF16 = jnp.bfloat16
VMEM = pl.BlockSpec(memory_space=pltpu.VMEM)
SMEM = pl.BlockSpec(memory_space=pltpu.SMEM)
HBM = pl.BlockSpec(memory_space=pltpu.HBM)
NT = (((1,), (1,)), ((), ()))
EPS = 1e-05
PARAMS = pltpu.CompilerParams(vmem_limit_bytes=24 * 1024 * 1024)


def silu(value):
    return value / (1.0 + jnp.exp(-value))


def pairs(steps):
    return [(t, r) for t in range(steps) for r in range(t + 1)]


def crossing_kernel(parent_hbm, state, window_hbm, out, parent, window, sems):
    slots = window.shape[1]
    nrows = state.shape[1]
    taps, _, width = window.shape
    groups = width // 128
    following = lax.axis_index("roll") + 1

    @pl.when(following == lax.axis_size("roll"))
    def _():
        out[...] = jnp.zeros(out.shape, BF16)

    @pl.when(following < lax.axis_size("roll"))
    def _():
        get_parent = pltpu.make_async_copy(parent_hbm, parent, sems.at[0])
        get_parent.start()
        get_window = pltpu.make_async_copy(window_hbm, window, sems.at[1])
        get_window.start()
        begin = following * slots
        get_parent.wait()
        row = jnp.int32(0)
        for s in range(slots):
            found = parent[begin + s] - begin + slots
            row = jnp.where(found < slots, found, row)
        row = jnp.clip(row, 0, slots - 1)
        copy = pltpu.make_async_copy(state.at[row], out.at[pl.ds(0, nrows)], sems.at[2])
        copy.start()
        pick = lax.broadcasted_iota(jnp.int32, (slots, 1), 0) == row
        place = lax.broadcasted_iota(jnp.int32, (out.shape[0] - nrows, 128), 0)
        packed = jnp.zeros(place.shape, F32)
        get_window.wait()
        for k in range(taps):
            chosen = jnp.sum(jnp.where(pick, window[k].astype(F32), 0.0), axis=0, keepdims=True)
            for j in range(groups):
                packed = jnp.where(place == k * groups + j, chosen[:, j * 128:(j + 1) * 128], packed)
        out[pl.ds(nrows, place.shape[0])] = packed.astype(BF16)
        copy.wait()


def local_kernel(
    parent, state, window, c_in, b_in, dt_raw, z_gate, conv, a_log, dt_bias, skip_d,
    base_out, reach_out, mix_out, conv_out, cmask_out, wmask_out,
):
    steps, slots, width = z_gate.shape
    heads = dt_raw.shape[1]
    taps = window.shape[0]
    nstate = c_in.shape[2]
    first = lax.axis_index("roll") * slots
    local = [parent[first + s] - first for s in range(slots)]
    held = [jnp.clip(row, 0, slots - 1) for row in local]

    slot_col = lax.broadcasted_iota(jnp.int32, (slots, slots), 0)
    slot_row = lax.broadcasted_iota(jnp.int32, (slots, slots), 1)
    choose = jnp.zeros((slots, slots), F32)
    slot_lane = lax.broadcasted_iota(jnp.int32, (slots, 128), 0)
    inside = jnp.zeros((slots, 128), F32)
    for s in range(slots):
        choose = jnp.where((slot_col == s) & (slot_row == local[s]), 1.0, choose)
        inside = jnp.where((slot_lane == s) & (local[s] >= 0), 1.0, inside)
    outside = 1.0 - inside
    wmask_out[...] = outside
    choose = choose.astype(BF16)

    taken = [jnp.dot(choose, window[k], preferred_element_type=F32) for k in range(taps)]
    weight = [conv[pl.ds(k, 1), :].astype(F32) for k in range(taps + 1)]
    for t in range(taps):
        part = weight[0] * taken[t]
        for k in range(1, taps - t):
            part = part + weight[k] * taken[t + k]
        conv_out[t] = part

    rate = jnp.exp(a_log[...])
    delta, decay = [], []
    for t in range(steps):
        raw = jnp.transpose(dt_raw[t]) + dt_bias[...]
        delta.append(jnp.maximum(raw, 0.0) + jnp.log1p(jnp.exp(-jnp.abs(raw))))
        decay.append(jnp.exp(-delta[t] * rate))
    c_rows = [c_in[t].astype(F32) for t in range(steps)]
    b_rows = [b_in[t].astype(F32) for t in range(steps)]
    coefs = []
    running = None
    for t in range(steps):
        running = decay[t] if running is None else running * decay[t]
        coefs.append(running)
    for t, r in pairs(steps):
        dot = jnp.sum(c_rows[t] * b_rows[r], axis=1, keepdims=True)
        coef = delta[r] * dot
        for j in range(r + 1, t + 1):
            coef = coef * decay[j]
        if t == r:
            coef = coef + skip_d[...]
        coefs.append(coef)
    stacked = jnp.concatenate(coefs, axis=0)
    head = lax.broadcasted_iota(jnp.int32, (heads, width), 0)
    lane_head = lax.broadcasted_iota(jnp.int32, (heads, width), 1) // (width // heads)
    expand = jnp.where(head == lane_head, 1.0, 0.0).astype(BF16)
    high = stacked.astype(BF16)
    low = (stacked - high.astype(F32)).astype(BF16)
    spread = jnp.dot(high, expand, preferred_element_type=F32) + jnp.dot(low, expand, preferred_element_type=F32)
    gate = [silu(z_gate[t].astype(F32)) for t in range(steps)]
    reach = []
    for t in range(steps):
        reach.append(spread[t * slots:(t + 1) * slots] * gate[t])
        reach_out[t] = reach[t]
    for i, (t, _) in enumerate(pairs(steps)):
        mix_out[i] = spread[(steps + i) * slots:(steps + i + 1) * slots] * gate[t]

    c_all = jnp.concatenate(c_rows, axis=0)
    slot_of = lax.rem(lax.broadcasted_iota(jnp.int32, (steps * slots, nstate), 0), slots)
    all_outside = jnp.concatenate([outside] * steps, axis=0)
    all_inside = 1.0 - all_outside
    cmask_out[...] = (c_all * all_outside).astype(BF16)
    c_inside = c_all * all_inside
    total = None
    for s in range(0, slots, 2):
        lhs = jnp.concatenate(
            [jnp.where(slot_of == s + i, c_inside, 0.0).astype(BF16) for i in range(2)], axis=1
        )
        rhs = jnp.concatenate([state[held[s]], state[held[s + 1]]], axis=1)
        part = lax.dot_general(lhs, rhs, NT, preferred_element_type=F32)
        total = part if total is None else total + part
    for t in range(steps):
        base_out[t] = total[t * slots:(t + 1) * slots] * reach[t]


def gated_rows(pre, base, mix, steps):
    inner = [silu(value) for value in pre]
    rows = list(base)
    for i, (t, r) in enumerate(pairs(steps)):
        rows[t] = rows[t] + mix[i] * inner[r]
    return rows


def square_sums(rows):
    squares = []
    for row in rows:
        sq = row * row
        part = sq[:, :128]
        for j in range(1, sq.shape[1] // 128):
            part = part + sq[:, j * 128:(j + 1) * 128]
        squares.append(part)
    flat = jnp.concatenate(squares, axis=0)
    flat = jnp.concatenate([flat, jnp.zeros((128 - flat.shape[0], 128), F32)], axis=0)
    return jnp.sum(jnp.transpose(flat), axis=0, keepdims=True)


def row_scales(parts, channels, rows):
    totals = jnp.sum(parts, axis=0)[:1]
    scale = lax.rsqrt(totals * (1.0 / channels) + EPS)
    return jnp.transpose(jnp.broadcast_to(scale, (128, 128)))[:rows]


def scaled(row, scale):
    return jnp.concatenate(
        [row[:, j * 128:(j + 1) * 128] * scale for j in range(row.shape[1] // 128)], axis=1
    )


def first_kernel(arrived, base, reach, mix, conv_part, cmask, wmask, conv, x_in, gain,
                 base_out, conv_out, send_out, sums_out):
    steps, slots, width = x_in.shape
    taps = conv_part.shape[0]
    nrows = arrived.shape[0] - 16
    groups = width // 128
    extra = lax.dot_general(cmask[...], arrived[pl.ds(0, nrows)], NT, preferred_element_type=F32)
    start = []
    for t in range(steps):
        start.append(base[t] + extra[t * slots:(t + 1) * slots] * reach[t])
        base_out[t] = start[t]
    packed = arrived[pl.ds(nrows, 16)].astype(F32)
    rows = [
        jnp.concatenate([packed[k * groups + j:k * groups + j + 1] for j in range(groups)], axis=1)
        for k in range(taps)
    ]
    weight = [conv[pl.ds(k, 1), :].astype(F32) for k in range(taps + 1)]
    mask = wmask[:, :1]
    pre = []
    for t in range(taps):
        part = weight[0] * rows[t]
        for k in range(1, taps - t):
            part = part + weight[k] * rows[t + k]
        pre.append(conv_part[t] + mask * part)
        conv_out[t] = pre[t]
    x_rows = [x_in[t].astype(F32) for t in range(steps)]
    pre = with_inputs(pre, weight, x_rows)
    gated = gated_rows(pre, start, [mix[i] for i in range(mix.shape[0])], steps)
    for t in range(steps):
        send_out[t] = gated[t] * gain[...]
    sums_out[...] = jnp.broadcast_to(square_sums(gated)[None], sums_out.shape)


def with_inputs(window_part, weight, x_rows):
    taps = len(window_part)
    pre = []
    for t in range(len(x_rows)):
        part = window_part[t] if t < taps else None
        for k in range(max(0, taps - t), taps + 1):
            term = weight[k] * x_rows[t + k - taps]
            part = term if part is None else part + term
        pre.append(part)
    return pre


def finish_kernel(sums, own, channels, out):
    steps, slots, _ = own.shape
    scale = row_scales(sums[...], channels, steps * slots)
    for t in range(steps):
        out[t] = scaled(own[t], scale[t * slots:(t + 1) * slots]).astype(BF16)


def second_kernel(sums, other, base, mix, conv_part, conv, channels, gated_out, sums_out):
    steps, slots, width = other.shape
    taps = conv_part.shape[0]
    scale = row_scales(sums[...], channels, steps * slots)
    rows = []
    for t in range(steps):
        row = scaled(other[t], scale[t * slots:(t + 1) * slots])
        rows.append(row.astype(BF16).astype(F32))
    weight = [conv[pl.ds(k, 1), :].astype(F32) for k in range(taps + 1)]
    pre = with_inputs([conv_part[t] for t in range(taps)], weight, rows)
    gated = gated_rows(pre, [base[t] for t in range(steps)], [mix[i] for i in range(mix.shape[0])], steps)
    for t in range(steps):
        gated_out[t] = gated[t]
    sums_out[...] = jnp.broadcast_to(square_sums(gated)[None], sums_out.shape)


def last_kernel(sums, gated, gain, channels, out):
    steps, slots, width = gated.shape
    scale = row_scales(sums[...], channels, steps * slots)
    for t in range(steps):
        out[t] = (scaled(gated[t], scale[t * slots:(t + 1) * slots]) * gain[...]).astype(BF16)


def body(ssm_state, conv_window, x_in, z_gate, dt_raw, b_in, c_in, conv_weight, a_log, dt_bias, skip_d, norm_gain, parent):
    _, slots, heads, head_dim, nstate = ssm_state.shape
    steps, _, width = x_in.shape
    taps = conv_window.shape[2]
    rows = heads * head_dim
    tp = lax.axis_size("tp")
    pipes = lax.axis_size("pipe")
    count = lax.axis_size("roll")
    channels = width * tp
    npairs = len(pairs(steps))
    state = ssm_state.reshape(slots, rows, nstate)
    window = jnp.transpose(conv_window[0], (1, 0, 2))
    raw = jnp.transpose(dt_raw[0], (0, 2, 1))
    shape = jax.ShapeDtypeStruct

    leaving = pl.pallas_call(
        crossing_kernel,
        out_shape=shape((rows + 16, nstate), BF16),
        in_specs=[HBM, HBM, HBM],
        out_specs=VMEM,
        scratch_shapes=[
            pltpu.SMEM(parent.shape, jnp.int32),
            pltpu.VMEM(window.shape, BF16),
            pltpu.SemaphoreType.DMA((3,)),
        ],
        compiler_params=PARAMS,
        name="crossing",
    )(*[pltpu.with_memory_space_constraint(value, pltpu.HBM) for value in (parent, state, window)])
    arrived = lax.ppermute(leaving, "roll", [(i, (i + 1) % count) for i in range(count)])

    base, reach, mix, conv_part, cmask, wmask = pl.pallas_call(
        local_kernel,
        out_shape=(
            shape((steps, slots, width), F32),
            shape((steps, slots, width), F32),
            shape((npairs, slots, width), F32),
            shape((taps, slots, width), F32),
            shape((steps * slots, nstate), BF16),
            shape((slots, 128), F32),
        ),
        in_specs=[SMEM] + [VMEM] * 10,
        out_specs=(VMEM,) * 6,
        compiler_params=PARAMS,
        cost_estimate=pl.CostEstimate(flops=20_000_000, bytes_accessed=4_000_000, transcendentals=0),
        name="local",
    )(parent, state, window, c_in[0], b_in[0], raw, z_gate[0], conv_weight[0], a_log, dt_bias, skip_d)

    base, conv_part, own, sums = pl.pallas_call(
        first_kernel,
        out_shape=(
            shape((steps, slots, width), F32),
            shape((taps, slots, width), F32),
            shape((steps, slots, width), F32),
            shape((pipes * tp, 1, 128), F32),
        ),
        in_specs=[VMEM] * 10,
        out_specs=(VMEM,) * 4,
        compiler_params=PARAMS,
        name="first",
    )(arrived, base, reach, mix, conv_part, cmask, wmask, conv_weight[0], x_in, norm_gain)
    other = lax.ppermute(own, "pipe", [(i, (i + 1) % pipes) for i in range(pipes)])
    section = lax.axis_index("pipe")
    sums, section = lax.optimization_barrier((sums, section))
    sums = lax.all_to_all(sums, ("pipe", "tp"), 0, 0)
    sums, section = lax.optimization_barrier((sums, section))

    def first_section(sums, own, other, base, mix, conv_part, conv, gain):
        return pl.pallas_call(
            lambda sums, own, out: finish_kernel(sums.at[pl.ds(0, tp)], own, channels, out),
            out_shape=shape((steps, slots, width), BF16),
            in_specs=[VMEM] * 2,
            out_specs=VMEM,
            compiler_params=PARAMS,
            name="finish",
        )(sums, own)

    def second_section(sums, own, other, base, mix, conv_part, conv, gain):
        gated, sums = pl.pallas_call(
            lambda sums, *refs: second_kernel(sums.at[pl.ds(0, tp)], *refs[:5], channels, *refs[5:]),
            out_shape=(shape((steps, slots, width), F32), shape((tp, 1, 128), F32)),
            in_specs=[VMEM] * 6,
            out_specs=(VMEM,) * 2,
            compiler_params=PARAMS,
            name="second",
        )(sums, other, base, mix, conv_part, conv)
        sums = lax.all_to_all(sums, "tp", 0, 0)
        return pl.pallas_call(
            lambda sums, gated, gain, out: last_kernel(sums, gated, gain, channels, out),
            out_shape=shape((steps, slots, width), BF16),
            in_specs=[VMEM] * 3,
            out_specs=VMEM,
            compiler_params=PARAMS,
            name="last",
        )(sums, gated, gain)

    result = lax.cond(
        section == 0, first_section, second_section,
        sums, own, other, base, mix, conv_part, conv_weight[0], norm_gain,
    )
    return result[None]


def solution(mesh):
    in_specs = (
        P("pipe", "roll", "tp", None, None),
        P("pipe", "roll", None, "tp"),
        P(None, "roll", "tp"),
        P("pipe", None, "roll", "tp"),
        P("pipe", None, "roll", "tp"),
        P("pipe", None, "roll", None),
        P("pipe", None, "roll", None),
        P("pipe", None, "tp"),
        P("pipe", "tp"),
        P("pipe", "tp"),
        P("pipe", "tp"),
        P("pipe", "tp"),
        P(),
    )
    out_specs = P("pipe", None, "roll", "tp")
    return jax.shard_map(body, mesh=mesh, in_specs=in_specs, out_specs=out_specs, check_vma=False)
```

```python
import jax
import jax.numpy as jnp
from jax import lax
from jax.experimental import pallas as pl
from jax.experimental.pallas import tpu as pltpu
from jax.sharding import PartitionSpec as P

F32 = jnp.float32
BF16 = jnp.bfloat16
VMEM = pl.BlockSpec(memory_space=pltpu.VMEM)
SMEM = pl.BlockSpec(memory_space=pltpu.SMEM)
HBM = pl.BlockSpec(memory_space=pltpu.HBM)
NT = (((1,), (1,)), ((), ()))
EPS = 1e-05
PARAMS = pltpu.CompilerParams(vmem_limit_bytes=24 * 1024 * 1024)


def silu(value):
    return value / (1.0 + jnp.exp(-value))


def pairs(steps):
    return [(t, r) for t in range(steps) for r in range(t + 1)]


def crossing_kernel(parent_hbm, state, window_hbm, out, parent, window, sems):
    slots = window.shape[1]
    nrows = state.shape[1]
    taps, _, width = window.shape
    groups = width // 128
    following = lax.axis_index("roll") + 1

    @pl.when(following == lax.axis_size("roll"))
    def _():
        out[...] = jnp.zeros(out.shape, BF16)

    @pl.when(following < lax.axis_size("roll"))
    def _():
        get_parent = pltpu.make_async_copy(parent_hbm, parent, sems.at[0])
        get_parent.start()
        get_window = pltpu.make_async_copy(window_hbm, window, sems.at[1])
        get_window.start()
        begin = following * slots
        get_parent.wait()
        row = jnp.int32(0)
        for s in range(slots):
            found = parent[begin + s] - begin + slots
            row = jnp.where(found < slots, found, row)
        row = jnp.clip(row, 0, slots - 1)
        copy = pltpu.make_async_copy(state.at[row], out.at[pl.ds(0, nrows)], sems.at[2])
        copy.start()
        pick = lax.broadcasted_iota(jnp.int32, (slots, 1), 0) == row
        place = lax.broadcasted_iota(jnp.int32, (out.shape[0] - nrows, 128), 0)
        packed = jnp.zeros(place.shape, F32)
        get_window.wait()
        for k in range(taps):
            chosen = jnp.sum(jnp.where(pick, window[k].astype(F32), 0.0), axis=0, keepdims=True)
            for j in range(groups):
                packed = jnp.where(place == k * groups + j, chosen[:, j * 128:(j + 1) * 128], packed)
        out[pl.ds(nrows, place.shape[0])] = packed.astype(BF16)
        copy.wait()


def local_kernel(
    parent, state, window, c_in, b_in, dt_raw, z_gate, conv, a_log, dt_bias, skip_d,
    base_out, reach_out, mix_out, conv_out, cmask_out, wmask_out,
):
    steps, slots, width = z_gate.shape
    heads = dt_raw.shape[1]
    taps = window.shape[0]
    nstate = c_in.shape[2]
    first = lax.axis_index("roll") * slots
    local = [parent[first + s] - first for s in range(slots)]
    held = [jnp.clip(row, 0, slots - 1) for row in local]

    slot_col = lax.broadcasted_iota(jnp.int32, (slots, slots), 0)
    slot_row = lax.broadcasted_iota(jnp.int32, (slots, slots), 1)
    choose = jnp.zeros((slots, slots), F32)
    slot_lane = lax.broadcasted_iota(jnp.int32, (slots, 128), 0)
    inside = jnp.zeros((slots, 128), F32)
    for s in range(slots):
        choose = jnp.where((slot_col == s) & (slot_row == local[s]), 1.0, choose)
        inside = jnp.where((slot_lane == s) & (local[s] >= 0), 1.0, inside)
    outside = 1.0 - inside
    wmask_out[...] = outside
    choose = choose.astype(BF16)

    taken = [jnp.dot(choose, window[k], preferred_element_type=F32) for k in range(taps)]
    weight = [conv[pl.ds(k, 1), :].astype(F32) for k in range(taps + 1)]
    for t in range(taps):
        part = weight[0] * taken[t]
        for k in range(1, taps - t):
            part = part + weight[k] * taken[t + k]
        conv_out[t] = part

    rate = jnp.exp(a_log[...])
    delta, decay = [], []
    for t in range(steps):
        raw = jnp.transpose(dt_raw[t]) + dt_bias[...]
        delta.append(jnp.maximum(raw, 0.0) + jnp.log1p(jnp.exp(-jnp.abs(raw))))
        decay.append(jnp.exp(-delta[t] * rate))
    c_rows = [c_in[t].astype(F32) for t in range(steps)]
    b_rows = [b_in[t].astype(F32) for t in range(steps)]
    coefs = []
    running = None
    for t in range(steps):
        running = decay[t] if running is None else running * decay[t]
        coefs.append(running)
    for t, r in pairs(steps):
        dot = jnp.sum(c_rows[t] * b_rows[r], axis=1, keepdims=True)
        coef = delta[r] * dot
        for j in range(r + 1, t + 1):
            coef = coef * decay[j]
        if t == r:
            coef = coef + skip_d[...]
        coefs.append(coef)
    stacked = jnp.concatenate(coefs, axis=0)
    head = lax.broadcasted_iota(jnp.int32, (heads, width), 0)
    lane_head = lax.broadcasted_iota(jnp.int32, (heads, width), 1) // (width // heads)
    expand = jnp.where(head == lane_head, 1.0, 0.0).astype(BF16)
    high = stacked.astype(BF16)
    low = (stacked - high.astype(F32)).astype(BF16)
    spread = jnp.dot(high, expand, preferred_element_type=F32) + jnp.dot(low, expand, preferred_element_type=F32)
    gate = [silu(z_gate[t].astype(F32)) for t in range(steps)]
    reach = []
    for t in range(steps):
        reach.append(spread[t * slots:(t + 1) * slots] * gate[t])
        reach_out[t] = reach[t]
    for i, (t, _) in enumerate(pairs(steps)):
        mix_out[i] = spread[(steps + i) * slots:(steps + i + 1) * slots] * gate[t]

    c_all = jnp.concatenate(c_rows, axis=0)
    slot_of = lax.rem(lax.broadcasted_iota(jnp.int32, (steps * slots, nstate), 0), slots)
    all_outside = jnp.concatenate([outside] * steps, axis=0)
    all_inside = 1.0 - all_outside
    cmask_out[...] = (c_all * all_outside).astype(BF16)
    c_inside = c_all * all_inside
    total = None
    for s in range(0, slots, 2):
        lhs = jnp.concatenate(
            [jnp.where(slot_of == s + i, c_inside, 0.0).astype(BF16) for i in range(2)], axis=1
        )
        rhs = jnp.concatenate([state[held[s]], state[held[s + 1]]], axis=1)
        part = lax.dot_general(lhs, rhs, NT, preferred_element_type=F32)
        total = part if total is None else total + part
    for t in range(steps):
        base_out[t] = total[t * slots:(t + 1) * slots] * reach[t]


def gated_rows(pre, base, mix, steps):
    inner = [silu(value) for value in pre]
    rows = list(base)
    for i, (t, r) in enumerate(pairs(steps)):
        rows[t] = rows[t] + mix[i] * inner[r]
    return rows


def square_sums(rows):
    squares = []
    for row in rows:
        sq = row * row
        part = sq[:, :128]
        for j in range(1, sq.shape[1] // 128):
            part = part + sq[:, j * 128:(j + 1) * 128]
        squares.append(part)
    flat = jnp.concatenate(squares, axis=0)
    flat = jnp.concatenate([flat, jnp.zeros((128 - flat.shape[0], 128), F32)], axis=0)
    return jnp.sum(jnp.transpose(flat), axis=0, keepdims=True)


def row_scales(parts, channels, rows):
    totals = jnp.sum(parts, axis=0)[:1]
    scale = lax.rsqrt(totals * (1.0 / channels) + EPS)
    return jnp.transpose(jnp.broadcast_to(scale, (128, 128)))[:rows]


def scaled(row, scale):
    return jnp.concatenate(
        [row[:, j * 128:(j + 1) * 128] * scale for j in range(row.shape[1] // 128)], axis=1
    )


def first_kernel(arrived, base, reach, mix, conv_part, cmask, wmask, conv, x_in, gain, *outs):
    base_out, conv_out, send_out, sums_out = outs
    steps, slots, width = x_in.shape
    taps = conv_part.shape[0]
    nrows = arrived.shape[0] - 16
    groups = width // 128
    extra = lax.dot_general(cmask[...], arrived[pl.ds(0, nrows)], NT, preferred_element_type=F32)
    start = []
    for t in range(steps):
        start.append(base[t] + extra[t * slots:(t + 1) * slots] * reach[t])
        base_out[t] = start[t]
    packed = arrived[pl.ds(nrows, 16)].astype(F32)
    rows = [
        jnp.concatenate([packed[k * groups + j:k * groups + j + 1] for j in range(groups)], axis=1)
        for k in range(taps)
    ]
    weight = [conv[pl.ds(k, 1), :].astype(F32) for k in range(taps + 1)]
    mask = wmask[:, :1]
    pre = []
    for t in range(taps):
        part = weight[0] * rows[t]
        for k in range(1, taps - t):
            part = part + weight[k] * rows[t + k]
        pre.append(conv_part[t] + mask * part)
        conv_out[t] = pre[t]
    send_first(pre, weight, start, mix, x_in, gain, send_out, sums_out)


def alone_kernel(base, mix, conv_part, conv, x_in, gain, send_out, sums_out):
    taps = conv_part.shape[0]
    weight = [conv[pl.ds(k, 1), :].astype(F32) for k in range(taps + 1)]
    start = [base[t] for t in range(base.shape[0])]
    send_first([conv_part[t] for t in range(taps)], weight, start, mix, x_in, gain, send_out, sums_out)


def send_first(pre, weight, start, mix, x_in, gain, send_out, sums_out):
    steps = x_in.shape[0]
    pre = with_inputs(pre, weight, [x_in[t].astype(F32) for t in range(steps)])
    gated = gated_rows(pre, start, [mix[i] for i in range(mix.shape[0])], steps)
    for t in range(steps):
        send_out[t] = gated[t] * gain[...]
    sums_out[...] = jnp.broadcast_to(square_sums(gated)[None], sums_out.shape)


def with_inputs(window_part, weight, x_rows):
    taps = len(window_part)
    pre = []
    for t in range(len(x_rows)):
        part = window_part[t] if t < taps else None
        for k in range(max(0, taps - t), taps + 1):
            term = weight[k] * x_rows[t + k - taps]
            part = term if part is None else part + term
        pre.append(part)
    return pre


def finish_kernel(sums, own, channels, out):
    steps, slots, _ = own.shape
    scale = row_scales(sums[...], channels, steps * slots)
    for t in range(steps):
        out[t] = scaled(own[t], scale[t * slots:(t + 1) * slots]).astype(BF16)


def second_kernel(sums, other, base, mix, conv_part, conv, channels, gated_out, sums_out):
    steps, slots, width = other.shape
    taps = conv_part.shape[0]
    scale = row_scales(sums[...], channels, steps * slots)
    rows = []
    for t in range(steps):
        row = scaled(other[t], scale[t * slots:(t + 1) * slots])
        rows.append(row.astype(BF16).astype(F32))
    weight = [conv[pl.ds(k, 1), :].astype(F32) for k in range(taps + 1)]
    pre = with_inputs([conv_part[t] for t in range(taps)], weight, rows)
    gated = gated_rows(pre, [base[t] for t in range(steps)], [mix[i] for i in range(mix.shape[0])], steps)
    for t in range(steps):
        gated_out[t] = gated[t]
    sums_out[...] = jnp.broadcast_to(square_sums(gated)[None], sums_out.shape)


def last_kernel(sums, gated, gain, channels, out):
    steps, slots, width = gated.shape
    scale = row_scales(sums[...], channels, steps * slots)
    for t in range(steps):
        out[t] = (scaled(gated[t], scale[t * slots:(t + 1) * slots]) * gain[...]).astype(BF16)


def body(ssm_state, conv_window, x_in, z_gate, dt_raw, b_in, c_in, conv_weight, a_log, dt_bias, skip_d, norm_gain, parent):
    _, slots, heads, head_dim, nstate = ssm_state.shape
    steps, _, width = x_in.shape
    taps = conv_window.shape[2]
    rows = heads * head_dim
    tp = lax.axis_size("tp")
    pipes = lax.axis_size("pipe")
    count = lax.axis_size("roll")
    channels = width * tp
    npairs = len(pairs(steps))
    state = ssm_state.reshape(slots, rows, nstate)
    window = jnp.transpose(conv_window[0], (1, 0, 2))
    raw = jnp.transpose(dt_raw[0], (0, 2, 1))
    shape = jax.ShapeDtypeStruct

    leaving = pl.pallas_call(
        crossing_kernel,
        out_shape=shape((rows + 16, nstate), BF16),
        in_specs=[HBM, HBM, HBM],
        out_specs=VMEM,
        scratch_shapes=[
            pltpu.SMEM(parent.shape, jnp.int32),
            pltpu.VMEM(window.shape, BF16),
            pltpu.SemaphoreType.DMA((3,)),
        ],
        compiler_params=PARAMS,
        name="crossing",
    )(*[pltpu.with_memory_space_constraint(value, pltpu.HBM) for value in (parent, state, window)])
    arrived = lax.ppermute(leaving, "roll", [(i, (i + 1) % count) for i in range(count)])

    base, reach, mix, conv_part, cmask, wmask = pl.pallas_call(
        local_kernel,
        out_shape=(
            shape((steps, slots, width), F32),
            shape((steps, slots, width), F32),
            shape((npairs, slots, width), F32),
            shape((taps, slots, width), F32),
            shape((steps * slots, nstate), BF16),
            shape((slots, 128), F32),
        ),
        in_specs=[SMEM] + [VMEM] * 10,
        out_specs=(VMEM,) * 6,
        compiler_params=PARAMS,
        cost_estimate=pl.CostEstimate(flops=20_000_000, bytes_accessed=4_000_000, transcendentals=0),
        name="local",
    )(parent, state, window, c_in[0], b_in[0], raw, z_gate[0], conv_weight[0], a_log, dt_bias, skip_d)

    def first_section(sums, own, other, base, mix, conv_part, conv, gain):
        return pl.pallas_call(
            lambda sums, own, out: finish_kernel(sums.at[pl.ds(0, tp)], own, channels, out),
            out_shape=shape((steps, slots, width), BF16),
            in_specs=[VMEM] * 2,
            out_specs=VMEM,
            compiler_params=PARAMS,
            name="finish",
        )(sums, own)

    def second_section(sums, own, other, base, mix, conv_part, conv, gain):
        gated, sums = pl.pallas_call(
            lambda sums, *refs: second_kernel(sums.at[pl.ds(0, tp)], *refs[:5], channels, *refs[5:]),
            out_shape=(shape((steps, slots, width), F32), shape((tp, 1, 128), F32)),
            in_specs=[VMEM] * 6,
            out_specs=(VMEM,) * 2,
            compiler_params=PARAMS,
            name="second",
        )(sums, other, base, mix, conv_part, conv)
        sums = lax.all_to_all(sums, "tp", 0, 0)
        return pl.pallas_call(
            lambda sums, gated, gain, out: last_kernel(sums, gated, gain, channels, out),
            out_shape=shape((steps, slots, width), BF16),
            in_specs=[VMEM] * 3,
            out_specs=VMEM,
            compiler_params=PARAMS,
            name="last",
        )(sums, gated, gain)

    def after_first(base, mix, conv_part, own, sums, conv, gain):
        other = lax.ppermute(own, "pipe", [(i, (i + 1) % pipes) for i in range(pipes)])
        section = lax.axis_index("pipe")
        sums, section = lax.optimization_barrier((sums, section))
        sums = lax.all_to_all(sums, ("pipe", "tp"), 0, 0)
        sums, section = lax.optimization_barrier((sums, section))
        return lax.cond(
            section == 0, first_section, second_section,
            sums, own, other, base, mix, conv_part, conv, gain,
        )

    sent = (shape((steps, slots, width), F32), shape((pipes * tp, 1, 128), F32))

    def alone(base, mix, conv_part, conv, x_in, gain):
        own, sums = pl.pallas_call(
            alone_kernel,
            out_shape=sent,
            in_specs=[VMEM] * 6,
            out_specs=(VMEM,) * 2,
            compiler_params=PARAMS,
            name="alone",
        )(base, mix, conv_part, conv, x_in, gain)
        return after_first(base, mix, conv_part, own, sums, conv, gain)

    def joined(early, arrived, base, reach, mix, conv_part, cmask, wmask, conv, x_in, gain):
        base, conv_part, own, sums = pl.pallas_call(
            first_kernel,
            out_shape=(shape((steps, slots, width), F32), shape((taps, slots, width), F32)) + sent,
            in_specs=[VMEM] * 10,
            out_specs=(VMEM,) * 4,
            compiler_params=PARAMS,
            name="first",
        )(arrived, base, reach, mix, conv_part, cmask, wmask, conv, x_in, gain)
        return after_first(base, mix, conv_part, own, sums, conv, gain)

    conv = conv_weight[0]
    lone = lax.axis_index("roll") == 0
    early = lax.cond(
        lone, alone, lambda base, mix, conv_part, conv, x_in, gain: x_in,
        base, mix, conv_part, conv, x_in, norm_gain,
    )
    result = lax.cond(
        lone, lambda early, *others: early, joined,
        early, arrived, base, reach, mix, conv_part, cmask, wmask, conv, x_in, norm_gain,
    )
    return result[None]


def solution(mesh):
    in_specs = (
        P("pipe", "roll", "tp", None, None),
        P("pipe", "roll", None, "tp"),
        P(None, "roll", "tp"),
        P("pipe", None, "roll", "tp"),
        P("pipe", None, "roll", "tp"),
        P("pipe", None, "roll", None),
        P("pipe", None, "roll", None),
        P("pipe", None, "tp"),
        P("pipe", "tp"),
        P("pipe", "tp"),
        P("pipe", "tp"),
        P("pipe", "tp"),
        P(),
    )
    out_specs = P("pipe", None, "roll", "tp")
    return jax.shard_map(body, mesh=mesh, in_specs=in_specs, out_specs=out_specs, check_vma=False)
```

```python
import jax
import jax.numpy as jnp
from jax import lax
from jax.experimental import pallas as pl
from jax.experimental.pallas import tpu as pltpu
from jax.sharding import PartitionSpec as P

F32 = jnp.float32
BF16 = jnp.bfloat16
VMEM = pl.BlockSpec(memory_space=pltpu.VMEM)
SMEM = pl.BlockSpec(memory_space=pltpu.SMEM)
HBM = pl.BlockSpec(memory_space=pltpu.HBM)
NT = (((1,), (1,)), ((), ()))
EPS = 1e-05
PARAMS = pltpu.CompilerParams(vmem_limit_bytes=24 * 1024 * 1024)


def silu(value):
    return value / (1.0 + jnp.exp(-value))


def tap_rows(conv):
    rows = conv[...].astype(F32)
    return [rows[k:k + 1] for k in range(rows.shape[0])]


def pairs(steps):
    return [(t, r) for t in range(steps) for r in range(t + 1)]


def crossing_row(parent, block, slots):
    begin = block * slots
    row = jnp.int32(0)
    for s in range(slots):
        found = parent[begin + s] - begin + slots
        row = jnp.where(found < slots, found, row)
    return jnp.clip(row, 0, slots - 1)


def packed_window(window, row):
    taps, slots, width = window.shape
    groups = width // 128
    pick = lax.broadcasted_iota(jnp.int32, (slots, 1), 0) == row
    place = lax.broadcasted_iota(jnp.int32, (16, 128), 0)
    packed = jnp.zeros(place.shape, F32)
    for k in range(taps):
        chosen = jnp.sum(jnp.where(pick, window[k].astype(F32), 0.0), axis=0, keepdims=True)
        for j in range(groups):
            packed = jnp.where(place == k * groups + j, chosen[:, j * 128:(j + 1) * 128], packed)
    return packed.astype(BF16)


def crossing_kernel(parent_hbm, state, window_hbm, out, parent, window, sems):
    slots = window.shape[1]
    nrows = state.shape[1]
    following = lax.axis_index("roll") + 1
    sends = (following < lax.axis_size("roll")) & (lax.axis_index("pipe") == 0)

    @pl.when(jnp.logical_not(sends))
    def _():
        out[...] = jnp.zeros(out.shape, BF16)

    @pl.when(sends)
    def _():
        get_parent = pltpu.make_async_copy(parent_hbm, parent, sems.at[0])
        get_parent.start()
        get_window = pltpu.make_async_copy(window_hbm, window, sems.at[1])
        get_window.start()
        get_parent.wait()
        row = crossing_row(parent, following, slots)
        copy = pltpu.make_async_copy(state.at[row], out.at[pl.ds(0, nrows)], sems.at[2])
        copy.start()
        get_window.wait()
        out[pl.ds(nrows, 16)] = packed_window(window, row)
        copy.wait()


def local_kernel(
    after, parent, state, window, c_in, b_in, dt_raw, z_gate, conv, a_log, dt_bias, skip_d,
    base_out, reach_out, mix_out, conv_out, cmask_out, wmask_out, leaving_out,
):
    steps, slots, width = z_gate.shape
    heads = dt_raw.shape[1]
    taps = window.shape[0]
    nstate = c_in.shape[2]
    roll = lax.axis_index("roll")
    first = roll * slots
    local = [parent[first + s] - first for s in range(slots)]
    held = [jnp.clip(row, 0, slots - 1) for row in local]

    slot_col = lax.broadcasted_iota(jnp.int32, (slots, slots), 0)
    slot_row = lax.broadcasted_iota(jnp.int32, (slots, slots), 1)
    choose = jnp.zeros((slots, slots), F32)
    slot_lane = lax.broadcasted_iota(jnp.int32, (slots, 128), 0)
    inside = jnp.zeros((slots, 128), F32)
    for s in range(slots):
        choose = jnp.where((slot_col == s) & (slot_row == local[s]), 1.0, choose)
        inside = jnp.where((slot_lane == s) & (local[s] >= 0), 1.0, inside)
    outside = 1.0 - inside
    wmask_out[...] = outside
    choose = choose.astype(BF16)

    taken = [jnp.dot(choose, window[k], preferred_element_type=F32) for k in range(taps)]
    weight = tap_rows(conv)
    for t in range(taps):
        part = weight[0] * taken[t]
        for k in range(1, taps - t):
            part = part + weight[k] * taken[t + k]
        conv_out[t] = part

    rate = jnp.exp(a_log[...])
    delta, decay = [], []
    for t in range(steps):
        raw = jnp.transpose(dt_raw[t]) + dt_bias[...]
        delta.append(jnp.maximum(raw, 0.0) + jnp.log1p(jnp.exp(-jnp.abs(raw))))
        decay.append(jnp.exp(-delta[t] * rate))
    c_rows = [c_in[t].astype(F32) for t in range(steps)]
    b_rows = [b_in[t].astype(F32) for t in range(steps)]
    coefs = []
    running = None
    for t in range(steps):
        running = decay[t] if running is None else running * decay[t]
        coefs.append(running)
    for t, r in pairs(steps):
        dot = jnp.sum(c_rows[t] * b_rows[r], axis=1, keepdims=True)
        coef = delta[r] * dot
        for j in range(r + 1, t + 1):
            coef = coef * decay[j]
        if t == r:
            coef = coef + skip_d[...]
        coefs.append(coef)
    stacked = jnp.concatenate(coefs, axis=0)
    head = lax.broadcasted_iota(jnp.int32, (heads, width), 0)
    lane_head = lax.broadcasted_iota(jnp.int32, (heads, width), 1) // (width // heads)
    expand = jnp.where(head == lane_head, 1.0, 0.0).astype(BF16)
    high = stacked.astype(BF16)
    low = (stacked - high.astype(F32)).astype(BF16)
    spread = jnp.dot(high, expand, preferred_element_type=F32) + jnp.dot(low, expand, preferred_element_type=F32)
    gate = [silu(z_gate[t].astype(F32)) for t in range(steps)]
    reach = []
    for t in range(steps):
        reach.append(spread[t * slots:(t + 1) * slots] * gate[t])
        reach_out[t] = reach[t]
    for i, (t, _) in enumerate(pairs(steps)):
        mix_out[i] = spread[(steps + i) * slots:(steps + i + 1) * slots] * gate[t]

    c_all = jnp.concatenate(c_rows, axis=0)
    slot_of = lax.rem(lax.broadcasted_iota(jnp.int32, (steps * slots, nstate), 0), slots)
    all_outside = jnp.concatenate([outside] * steps, axis=0)
    all_inside = 1.0 - all_outside
    cmask_out[...] = (c_all * all_outside).astype(BF16)
    c_inside = c_all * all_inside
    total = None
    for s in range(0, slots, 2):
        lhs = jnp.concatenate(
            [jnp.where(slot_of == s + i, c_inside, 0.0).astype(BF16) for i in range(2)], axis=1
        )
        rhs = jnp.concatenate([state[held[s]], state[held[s + 1]]], axis=1)
        part = lax.dot_general(lhs, rhs, NT, preferred_element_type=F32)
        total = part if total is None else total + part
    for t in range(steps):
        base_out[t] = total[t * slots:(t + 1) * slots] * reach[t]

    row = crossing_row(parent, lax.rem(roll + 1, lax.axis_size("roll")), slots)
    nrows = state.shape[1]
    leaving_out[pl.ds(0, nrows)] = state[row]
    leaving_out[pl.ds(nrows, 16)] = packed_window(window, row)


def gated_rows(pre, base, mix, steps):
    inner = [silu(value) for value in pre]
    rows = list(base)
    for i, (t, r) in enumerate(pairs(steps)):
        rows[t] = rows[t] + mix[i] * inner[r]
    return rows


def square_sums(rows):
    squares = []
    for row in rows:
        sq = row * row
        part = sq[:, :128]
        for j in range(1, sq.shape[1] // 128):
            part = part + sq[:, j * 128:(j + 1) * 128]
        squares.append(part)
    flat = jnp.concatenate(squares, axis=0)
    flat = jnp.concatenate([flat, jnp.zeros((128 - flat.shape[0], 128), F32)], axis=0)
    return jnp.sum(jnp.transpose(flat), axis=0, keepdims=True)


def row_scales(parts, channels, rows):
    totals = jnp.sum(parts, axis=0)[:1]
    scale = lax.rsqrt(totals * (1.0 / channels) + EPS)
    return jnp.transpose(jnp.broadcast_to(scale, (128, 128)))[:rows]


def scaled(row, scale):
    return jnp.concatenate(
        [row[:, j * 128:(j + 1) * 128] * scale for j in range(row.shape[1] // 128)], axis=1
    )


def with_inputs(window_part, weight, x_rows):
    taps = len(window_part)
    pre = []
    for t in range(len(x_rows)):
        part = window_part[t] if t < taps else None
        for k in range(max(0, taps - t), taps + 1):
            term = weight[k] * x_rows[t + k - taps]
            part = term if part is None else part + term
        pre.append(part)
    return pre


def arrived_rows(arrived, taps, groups):
    nrows = arrived.shape[0] - 16
    packed = arrived[pl.ds(nrows, 16)].astype(F32)
    rows = [
        jnp.concatenate([packed[k * groups + j:k * groups + j + 1] for j in range(groups)], axis=1)
        for k in range(taps)
    ]
    return arrived[pl.ds(0, nrows)], rows


def window_terms(weight, rows):
    taps = len(rows)
    parts = []
    for t in range(taps):
        part = weight[0] * rows[t]
        for k in range(1, taps - t):
            part = part + weight[k] * rows[t + k]
        parts.append(part)
    return parts


def front_kernel(base, reach, mix, conv_part, cmask, wmask, conv, x_in, gain, pack_out, extra_out, row_out):
    steps, slots, width = x_in.shape
    taps = conv_part.shape[0]
    outside = wmask[:, :1]
    weight = tap_rows(conv)
    pre = with_inputs([conv_part[t] for t in range(taps)], weight, [x_in[t].astype(F32) for t in range(steps)])
    count = mix.shape[0]
    mixes = [mix[i] for i in range(count)]
    gated = gated_rows(pre, [base[t] for t in range(steps)], mixes, steps)
    gated = [row * (1.0 - outside) for row in gated]
    for t in range(steps):
        pack_out[pl.ds(t * slots, slots)] = gated[t] * gain[...]

    def crossing(value):
        return jnp.sum(value * outside, axis=0, keepdims=True)

    slot_c = [jnp.sum(cmask[pl.ds(t * slots, slots)].astype(F32), axis=0, keepdims=True) for t in range(steps)]
    rows = [crossing(reach[t]) for t in range(steps)]
    rows += [crossing(value) for value in mixes]
    rows += [crossing(value) for value in pre]
    rows += weight + [gain[...], jnp.concatenate(slot_c, axis=1)]
    extra_out[...] = jnp.concatenate(rows + [jnp.zeros_like(gain)] * (extra_out.shape[0] - len(rows)), axis=0)
    lane = lax.broadcasted_iota(jnp.int32, (slots, 128), 1)
    slot = lax.broadcasted_iota(jnp.int32, (slots, 128), 0)
    lanes = jnp.sum(jnp.where(lax.rem(lane, slots) == slot, wmask[...], 0.0), axis=0, keepdims=True)
    row_out[...] = jnp.concatenate([square_sums(gated), lanes, jnp.zeros((6, 128), F32)], axis=0)


def fill_kernel(arrived, pack, extra, row, wmask, taps, other_out, sums_out):
    steps, slots, width = other_out.shape
    number = len(pairs(steps))
    nstate = arrived.shape[1]
    extra = extra[...]

    def take(begin, size):
        return [extra[begin + i:begin + i + 1] for i in range(size)]

    reach = take(0, steps)
    mixes = take(steps, number)
    pre = take(steps + number, steps)
    weight = take(2 * steps + number, taps + 1)
    gain, slot_c = take(2 * steps + number + taps + 1, 2)
    state, rows = arrived_rows(arrived, taps, width // 128)
    lhs = [slot_c[:, t * nstate:(t + 1) * nstate] for t in range(steps)]
    lhs = jnp.concatenate(lhs + [jnp.zeros((16 - steps, nstate), F32)], axis=0).astype(BF16)
    start = lax.dot_general(lhs, state, NT, preferred_element_type=F32)
    for t, term in enumerate(window_terms(weight, rows)):
        pre[t] = pre[t] + term
    gated = gated_rows(pre, [start[t:t + 1] * reach[t] for t in range(steps)], mixes, steps)
    mask = wmask[:, :1]
    lane = lax.broadcasted_iota(jnp.int32, (1, 128), 1)
    sums = jnp.zeros((1, 128), F32)
    for t in range(steps):
        other_out[t] = pack[pl.ds(t * slots, slots)] + mask * (gated[t] * gain)
        square = jnp.sum(gated[t] * gated[t], axis=1, keepdims=True)
        here = (lane >= t * slots) & (lane < (t + 1) * slots)
        sums = jnp.where(here, square, sums)
    sums = jnp.where(lax.axis_index("pipe") == 0, row[pl.ds(0, 1)], sums * row[pl.ds(1, 1)])
    sums_out[...] = jnp.broadcast_to(sums[None], sums_out.shape)


def finish_kernel(sums, own, channels, out):
    steps, slots, _ = out.shape
    scale = row_scales(sums[...], channels, steps * slots)
    for t in range(steps):
        out[t] = scaled(own[t], scale[t * slots:(t + 1) * slots]).astype(BF16)


def second_kernel(
    sums, other, arrived, base, reach, mix, conv_part, cmask, wmask, conv, channels, gated_out, sums_out
):
    steps, slots, width = other.shape
    taps = conv_part.shape[0]
    weight = tap_rows(conv)
    state, rows = arrived_rows(arrived, taps, width // 128)
    extra = lax.dot_general(cmask[...], state, NT, preferred_element_type=F32)
    start = [base[t] + extra[t * slots:(t + 1) * slots] * reach[t] for t in range(steps)]
    mask = wmask[:, :1]
    pre = [conv_part[t] + mask * term for t, term in enumerate(window_terms(weight, rows))]
    scale = row_scales(sums[...], channels, steps * slots)
    inputs = [
        scaled(other[t], scale[t * slots:(t + 1) * slots]).astype(BF16).astype(F32) for t in range(steps)
    ]
    pre = with_inputs(pre, weight, inputs)
    gated = gated_rows(pre, start, [mix[i] for i in range(mix.shape[0])], steps)
    for t in range(steps):
        gated_out[t] = gated[t]
    sums_out[...] = jnp.broadcast_to(square_sums(gated)[None], sums_out.shape)


def last_kernel(sums, gated, gain, channels, out):
    steps, slots, width = gated.shape
    scale = row_scales(sums[...], channels, steps * slots)
    for t in range(steps):
        out[t] = (scaled(gated[t], scale[t * slots:(t + 1) * slots]) * gain[...]).astype(BF16)


def body(ssm_state, conv_window, x_in, z_gate, dt_raw, b_in, c_in, conv_weight, a_log, dt_bias, skip_d, norm_gain, parent):
    _, slots, heads, head_dim, nstate = ssm_state.shape
    steps, _, width = x_in.shape
    taps = conv_window.shape[2]
    rows = heads * head_dim
    tp = lax.axis_size("tp")
    pipes = lax.axis_size("pipe")
    count = lax.axis_size("roll")
    channels = width * tp
    npairs = len(pairs(steps))
    state = ssm_state.reshape(slots, rows, nstate)
    window = jnp.transpose(conv_window[0], (1, 0, 2))
    raw = jnp.transpose(dt_raw[0], (0, 2, 1))
    conv = conv_weight[0]
    shape = jax.ShapeDtypeStruct
    step_rows = shape((steps, slots, width), F32)
    packed_slot = shape((rows + 16, nstate), BF16)
    nextra = (2 * steps + npairs + taps + 3 + 7) // 8 * 8

    def at(i, p, t):
        return (i * pipes + p) * tp + t

    end = count - 1
    first_moves, second_moves = [], []
    for t in range(tp):
        first_moves += [(at(i, 0, t), at(i + 1, 1, t)) for i in range(end)]
        first_moves += [(at(i + 1, 1, t), at(i, 0, t)) for i in range(end)]
        first_moves += [(at(end, 0, t), at(end, 0, t ^ 1)), (at(0, 1, t), at(0, 1, t ^ 1))]
        second_moves += [(at(i, 1, t), at(i + 1, 1, t)) for i in range(end)]
        second_moves += [(at(i + 1, 0, t), at(i, 0, t)) for i in range(end)]
        second_moves += [(at(end, 1, t), at(end, 0, t)), (at(0, 0, t), at(0, 1, t))]
    swap = [(i, (i + 1) % pipes) for i in range(pipes)]

    leaving = pl.pallas_call(
        crossing_kernel,
        out_shape=packed_slot,
        in_specs=[HBM, HBM, HBM],
        out_specs=VMEM,
        scratch_shapes=[
            pltpu.SMEM(parent.shape, jnp.int32),
            pltpu.VMEM(window.shape, BF16),
            pltpu.SemaphoreType.DMA((3,)),
        ],
        compiler_params=PARAMS,
        name="crossing",
    )(*[pltpu.with_memory_space_constraint(value, pltpu.HBM) for value in (parent, state, window)])
    arrived = lax.ppermute(leaving, ("roll", "pipe", "tp"), first_moves)

    base, reach, mix, conv_part, cmask, wmask, leaving = pl.pallas_call(
        local_kernel,
        out_shape=(
            step_rows,
            step_rows,
            shape((npairs, slots, width), F32),
            shape((taps, slots, width), F32),
            shape((steps * slots, nstate), BF16),
            shape((slots, 128), F32),
            packed_slot,
        ),
        in_specs=[HBM, SMEM] + [VMEM] * 10,
        out_specs=(VMEM,) * 7,
        compiler_params=PARAMS,
        cost_estimate=pl.CostEstimate(flops=20_000_000, bytes_accessed=4_000_000, transcendentals=0),
        name="local",
    )(leaving, parent, state, window, c_in[0], b_in[0], raw, z_gate[0], conv, a_log, dt_bias, skip_d)

    pack, extra, row = pl.pallas_call(
        front_kernel,
        out_shape=(shape((steps * slots, width), F32), shape((nextra, width), F32), shape((8, 128), F32)),
        in_specs=[VMEM] * 9,
        out_specs=(VMEM,) * 3,
        compiler_params=PARAMS,
        name="front",
    )(base, reach, mix, conv_part, cmask, wmask, conv, x_in, norm_gain)
    other_extra = lax.ppermute(extra, "pipe", swap)
    other_pack = lax.ppermute(pack, "pipe", swap)
    later = lax.ppermute(leaving, ("roll", "pipe", "tp"), second_moves)

    whole, sums = pl.pallas_call(
        lambda *refs: fill_kernel(*refs[:5], taps, *refs[5:]),
        out_shape=(step_rows, shape((pipes * tp, 1, 128), F32)),
        in_specs=[VMEM] * 5,
        out_specs=(VMEM,) * 2,
        compiler_params=PARAMS,
        name="fill",
    )(arrived, other_pack, other_extra, row, wmask)
    other_whole = lax.ppermute(whole, "pipe", swap)
    section = lax.axis_index("pipe")
    sums, section = lax.optimization_barrier((sums, section))
    sums = lax.all_to_all(sums, ("pipe", "tp"), 0, 0)
    sums, section = lax.optimization_barrier((sums, section))

    def first_section(sums, other_whole, whole, later, base, reach, mix, conv_part, cmask, wmask, conv, gain):
        return pl.pallas_call(
            lambda sums, own, out: finish_kernel(sums, own, channels, out),
            out_shape=shape((steps, slots, width), BF16),
            in_specs=[VMEM] * 2,
            out_specs=VMEM,
            compiler_params=PARAMS,
            name="finish",
        )(sums, other_whole)

    def second_section(sums, other_whole, whole, later, base, reach, mix, conv_part, cmask, wmask, conv, gain):
        gated, sums = pl.pallas_call(
            lambda *refs: second_kernel(*refs[:10], channels, *refs[10:]),
            out_shape=(step_rows, shape((tp, 1, 128), F32)),
            in_specs=[VMEM] * 10,
            out_specs=(VMEM,) * 2,
            compiler_params=PARAMS,
            name="second",
        )(sums, whole, later, base, reach, mix, conv_part, cmask, wmask, conv)
        sums = lax.all_to_all(sums, "tp", 0, 0)
        return pl.pallas_call(
            lambda sums, gated, gain, out: last_kernel(sums, gated, gain, channels, out),
            out_shape=shape((steps, slots, width), BF16),
            in_specs=[VMEM] * 3,
            out_specs=VMEM,
            compiler_params=PARAMS,
            name="last",
        )(sums, gated, gain)

    result = lax.cond(
        section == 0, first_section, second_section,
        sums, other_whole, whole, later, base, reach, mix, conv_part, cmask, wmask, conv, norm_gain,
    )
    return result[None]


def solution(mesh):
    in_specs = (
        P("pipe", "roll", "tp", None, None),
        P("pipe", "roll", None, "tp"),
        P(None, "roll", "tp"),
        P("pipe", None, "roll", "tp"),
        P("pipe", None, "roll", "tp"),
        P("pipe", None, "roll", None),
        P("pipe", None, "roll", None),
        P("pipe", None, "tp"),
        P("pipe", "tp"),
        P("pipe", "tp"),
        P("pipe", "tp"),
        P("pipe", "tp"),
        P(),
    )
    out_specs = P("pipe", None, "roll", "tp")
    return jax.shard_map(body, mesh=mesh, in_specs=in_specs, out_specs=out_specs, check_vma=False)
```

```python
import jax
import jax.numpy as jnp
from jax import lax
from jax.experimental import pallas as pl
from jax.experimental.pallas import tpu as pltpu
from jax.sharding import PartitionSpec as P

F32 = jnp.float32
BF16 = jnp.bfloat16
VMEM = pl.BlockSpec(memory_space=pltpu.VMEM)
SMEM = pl.BlockSpec(memory_space=pltpu.SMEM)
HBM = pl.BlockSpec(memory_space=pltpu.HBM)
NT = (((1,), (1,)), ((), ()))
EPS = 1e-05
PARAMS = pltpu.CompilerParams(vmem_limit_bytes=24 * 1024 * 1024)


def silu(value):
    return value / (1.0 + jnp.exp(-value))


def tap_rows(conv):
    rows = conv[...].astype(F32)
    return [rows[k:k + 1] for k in range(rows.shape[0])]


def pairs(steps):
    return [(t, r) for t in range(steps) for r in range(t + 1)]


def crossing_row(parent, block, slots):
    begin = block * slots
    row = jnp.int32(0)
    for s in range(slots):
        found = parent[begin + s] - begin + slots
        row = jnp.where(found < slots, found, row)
    return jnp.clip(row, 0, slots - 1)


def packed_window(window, row):
    taps, slots, width = window.shape
    groups = width // 128
    pick = lax.broadcasted_iota(jnp.int32, (slots, 1), 0) == row
    place = lax.broadcasted_iota(jnp.int32, (16, 128), 0)
    packed = jnp.zeros(place.shape, F32)
    for k in range(taps):
        chosen = jnp.sum(jnp.where(pick, window[k].astype(F32), 0.0), axis=0, keepdims=True)
        for j in range(groups):
            packed = jnp.where(place == k * groups + j, chosen[:, j * 128:(j + 1) * 128], packed)
    return packed.astype(BF16)


def crossing_kernel(parent_hbm, state, window_hbm, out, parent, window, sems):
    slots = window.shape[1]
    nrows = state.shape[1]
    following = lax.axis_index("roll") + 1
    sends = (following < lax.axis_size("roll")) & (lax.axis_index("pipe") == 0)

    @pl.when(jnp.logical_not(sends))
    def _():
        out[...] = jnp.zeros(out.shape, BF16)

    @pl.when(sends)
    def _():
        get_parent = pltpu.make_async_copy(parent_hbm, parent, sems.at[0])
        get_parent.start()
        get_window = pltpu.make_async_copy(window_hbm, window, sems.at[1])
        get_window.start()
        get_parent.wait()
        row = crossing_row(parent, following, slots)
        copy = pltpu.make_async_copy(state.at[row], out.at[pl.ds(0, nrows)], sems.at[2])
        copy.start()
        get_window.wait()
        out[pl.ds(nrows, 16)] = packed_window(window, row)
        copy.wait()


def local_kernel(
    after, parent, state, window, c_in, b_in, dt_raw, z_gate, conv, a_log, dt_bias, skip_d,
    base_out, reach_out, mix_out, conv_out, cmask_out, wmask_out, leaving_out,
):
    steps, slots, width = z_gate.shape
    heads = dt_raw.shape[1]
    taps = window.shape[0]
    nstate = c_in.shape[2]
    roll = lax.axis_index("roll")
    first = roll * slots
    local = [parent[first + s] - first for s in range(slots)]
    held = [jnp.clip(row, 0, slots - 1) for row in local]

    slot_col = lax.broadcasted_iota(jnp.int32, (slots, slots), 0)
    slot_row = lax.broadcasted_iota(jnp.int32, (slots, slots), 1)
    choose = jnp.zeros((slots, slots), F32)
    slot_lane = lax.broadcasted_iota(jnp.int32, (slots, 128), 0)
    inside = jnp.zeros((slots, 128), F32)
    for s in range(slots):
        choose = jnp.where((slot_col == s) & (slot_row == local[s]), 1.0, choose)
        inside = jnp.where((slot_lane == s) & (local[s] >= 0), 1.0, inside)
    outside = 1.0 - inside
    wmask_out[...] = outside
    choose = choose.astype(BF16)

    taken = [jnp.dot(choose, window[k], preferred_element_type=F32) for k in range(taps)]
    weight = tap_rows(conv)
    for t in range(taps):
        part = weight[0] * taken[t]
        for k in range(1, taps - t):
            part = part + weight[k] * taken[t + k]
        conv_out[t] = part

    rate = jnp.exp(a_log[...])
    delta, decay = [], []
    for t in range(steps):
        raw = jnp.transpose(dt_raw[t]) + dt_bias[...]
        delta.append(jnp.maximum(raw, 0.0) + jnp.log1p(jnp.exp(-jnp.abs(raw))))
        decay.append(jnp.exp(-delta[t] * rate))
    c_rows = [c_in[t].astype(F32) for t in range(steps)]
    b_rows = [b_in[t].astype(F32) for t in range(steps)]
    coefs = []
    running = None
    for t in range(steps):
        running = decay[t] if running is None else running * decay[t]
        coefs.append(running)
    for t, r in pairs(steps):
        dot = jnp.sum(c_rows[t] * b_rows[r], axis=1, keepdims=True)
        coef = delta[r] * dot
        for j in range(r + 1, t + 1):
            coef = coef * decay[j]
        if t == r:
            coef = coef + skip_d[...]
        coefs.append(coef)
    stacked = jnp.concatenate(coefs, axis=0)
    head = lax.broadcasted_iota(jnp.int32, (heads, width), 0)
    lane_head = lax.broadcasted_iota(jnp.int32, (heads, width), 1) // (width // heads)
    expand = jnp.where(head == lane_head, 1.0, 0.0).astype(BF16)
    high = stacked.astype(BF16)
    low = (stacked - high.astype(F32)).astype(BF16)
    spread = jnp.dot(high, expand, preferred_element_type=F32) + jnp.dot(low, expand, preferred_element_type=F32)
    gate = [silu(z_gate[t].astype(F32)) for t in range(steps)]
    reach = []
    for t in range(steps):
        reach.append(spread[t * slots:(t + 1) * slots] * gate[t])
        reach_out[t] = reach[t]
    for i, (t, _) in enumerate(pairs(steps)):
        mix_out[i] = spread[(steps + i) * slots:(steps + i + 1) * slots] * gate[t]

    c_all = jnp.concatenate(c_rows, axis=0)
    slot_of = lax.rem(lax.broadcasted_iota(jnp.int32, (steps * slots, nstate), 0), slots)
    all_outside = jnp.concatenate([outside] * steps, axis=0)
    all_inside = 1.0 - all_outside
    cmask_out[...] = (c_all * all_outside).astype(BF16)
    c_inside = c_all * all_inside
    total = None
    for s in range(0, slots, 2):
        lhs = jnp.concatenate(
            [jnp.where(slot_of == s + i, c_inside, 0.0).astype(BF16) for i in range(2)], axis=1
        )
        rhs = jnp.concatenate([state[held[s]], state[held[s + 1]]], axis=1)
        part = lax.dot_general(lhs, rhs, NT, preferred_element_type=F32)
        total = part if total is None else total + part
    for t in range(steps):
        base_out[t] = total[t * slots:(t + 1) * slots] * reach[t]

    row = crossing_row(parent, lax.rem(roll + 1, lax.axis_size("roll")), slots)
    nrows = state.shape[1]
    leaving_out[pl.ds(0, nrows)] = state[row]
    leaving_out[pl.ds(nrows, 16)] = packed_window(window, row)


def gated_rows(pre, base, mix, steps):
    inner = [silu(value) for value in pre]
    rows = list(base)
    for i, (t, r) in enumerate(pairs(steps)):
        rows[t] = rows[t] + mix[i] * inner[r]
    return rows


def square_sums(rows):
    squares = []
    for row in rows:
        sq = row * row
        part = sq[:, :128]
        for j in range(1, sq.shape[1] // 128):
            part = part + sq[:, j * 128:(j + 1) * 128]
        squares.append(part)
    flat = jnp.concatenate(squares, axis=0)
    flat = jnp.concatenate([flat, jnp.zeros((128 - flat.shape[0], 128), F32)], axis=0)
    return jnp.sum(jnp.transpose(flat), axis=0, keepdims=True)


def row_scales(parts, channels, rows):
    totals = jnp.sum(parts, axis=0)[:1]
    scale = lax.rsqrt(totals * (1.0 / channels) + EPS)
    return jnp.transpose(jnp.broadcast_to(scale, (128, 128)))[:rows]


def scaled(row, scale):
    return jnp.concatenate(
        [row[:, j * 128:(j + 1) * 128] * scale for j in range(row.shape[1] // 128)], axis=1
    )


def with_inputs(window_part, weight, x_rows):
    taps = len(window_part)
    pre = []
    for t in range(len(x_rows)):
        part = window_part[t] if t < taps else None
        for k in range(max(0, taps - t), taps + 1):
            term = weight[k] * x_rows[t + k - taps]
            part = term if part is None else part + term
        pre.append(part)
    return pre


def arrived_rows(arrived, taps, groups):
    nrows = arrived.shape[0] - 16
    packed = arrived[pl.ds(nrows, 16)].astype(F32)
    rows = [
        jnp.concatenate([packed[k * groups + j:k * groups + j + 1] for j in range(groups)], axis=1)
        for k in range(taps)
    ]
    return arrived[pl.ds(0, nrows)], rows


def window_terms(weight, rows):
    taps = len(rows)
    parts = []
    for t in range(taps):
        part = weight[0] * rows[t]
        for k in range(1, taps - t):
            part = part + weight[k] * rows[t + k]
        parts.append(part)
    return parts


def front_kernel(base, reach, mix, conv_part, cmask, wmask, conv, x_in, gain, pack_out, extra_out, row_out):
    steps, slots, width = x_in.shape
    taps = conv_part.shape[0]
    lane = lax.broadcasted_iota(jnp.int32, (slots, 128), 1)
    slot = lax.broadcasted_iota(jnp.int32, (slots, 128), 0)
    lanes = jnp.sum(jnp.where(lax.rem(lane, slots) == slot, wmask[...], 0.0), axis=0, keepdims=True)
    row_out[...] = jnp.broadcast_to(lanes, row_out.shape)

    @pl.when(lax.axis_index("pipe") > 0)
    def _():
        pack_out[...] = jnp.zeros(pack_out.shape, F32)
        extra_out[...] = jnp.zeros(extra_out.shape, F32)

    @pl.when(lax.axis_index("pipe") == 0)
    def _():
        outside = wmask[:, :1]
        weight = tap_rows(conv)
        pre = with_inputs([conv_part[t] for t in range(taps)], weight, [x_in[t].astype(F32) for t in range(steps)])
        count = mix.shape[0]
        mixes = [mix[i] for i in range(count)]
        gated = gated_rows(pre, [base[t] for t in range(steps)], mixes, steps)
        gated = [row * (1.0 - outside) for row in gated]
        for t in range(steps):
            pack_out[pl.ds(t * slots, slots)] = gated[t] * gain[...]

        def crossing(value):
            return jnp.sum(value * outside, axis=0, keepdims=True)

        slot_c = [jnp.sum(cmask[pl.ds(t * slots, slots)].astype(F32), axis=0, keepdims=True) for t in range(steps)]
        rows = [crossing(reach[t]) for t in range(steps)]
        rows += [crossing(value) for value in mixes]
        rows += [crossing(value) for value in pre]
        rows += weight + [gain[...], jnp.concatenate(slot_c, axis=1)]
        rows.append(jnp.concatenate([square_sums(gated), jnp.zeros((1, width - 128), F32)], axis=1))
        blank = jnp.zeros((extra_out.shape[0] - len(rows), width), F32)
        extra_out[...] = jnp.concatenate(rows + [blank], axis=0)


def fill_kernel(arrived, pack, extra, row, wmask, taps, other_out, sums_out):
    steps, slots, width = other_out.shape
    number = len(pairs(steps))
    nstate = arrived.shape[1]
    extra = extra[...]

    def take(begin, size):
        return [extra[begin + i:begin + i + 1] for i in range(size)]

    reach = take(0, steps)
    mixes = take(steps, number)
    pre = take(steps + number, steps)
    weight = take(2 * steps + number, taps + 1)
    gain, slot_c, local = take(2 * steps + number + taps + 1, 3)
    state, rows = arrived_rows(arrived, taps, width // 128)
    lhs = [slot_c[:, t * nstate:(t + 1) * nstate] for t in range(steps)]
    lhs = jnp.concatenate(lhs + [jnp.zeros((16 - steps, nstate), F32)], axis=0).astype(BF16)
    start = lax.dot_general(lhs, state, NT, preferred_element_type=F32)
    for t, term in enumerate(window_terms(weight, rows)):
        pre[t] = pre[t] + term
    gated = gated_rows(pre, [start[t:t + 1] * reach[t] for t in range(steps)], mixes, steps)
    mask = wmask[:, :1]
    lane = lax.broadcasted_iota(jnp.int32, (1, 128), 1)
    sums = jnp.zeros((1, 128), F32)
    for t in range(steps):
        other_out[t] = pack[pl.ds(t * slots, slots)] + mask * (gated[t] * gain)
        square = jnp.sum(gated[t] * gated[t], axis=1, keepdims=True)
        here = (lane >= t * slots) & (lane < (t + 1) * slots)
        sums = jnp.where(here, square, sums)
    sums = local[:, :128] + sums * row[pl.ds(0, 1)]
    sums_out[...] = jnp.broadcast_to(sums[None], sums_out.shape)


def second_kernel(
    sums, other, arrived, base, reach, mix, conv_part, cmask, wmask, conv, channels, norm_out, gated_out, sums_out
):
    steps, slots, width = other.shape
    taps = conv_part.shape[0]
    weight = tap_rows(conv)
    state, rows = arrived_rows(arrived, taps, width // 128)
    extra = lax.dot_general(cmask[...], state, NT, preferred_element_type=F32)
    start = [base[t] + extra[t * slots:(t + 1) * slots] * reach[t] for t in range(steps)]
    mask = wmask[:, :1]
    pre = [conv_part[t] + mask * term for t, term in enumerate(window_terms(weight, rows))]
    scale = row_scales(sums[...], channels, steps * slots)
    inputs = []
    for t in range(steps):
        row = scaled(other[t], scale[t * slots:(t + 1) * slots]).astype(BF16)
        norm_out[t] = row
        inputs.append(row.astype(F32))
    pre = with_inputs(pre, weight, inputs)
    gated = gated_rows(pre, start, [mix[i] for i in range(mix.shape[0])], steps)
    for t in range(steps):
        gated_out[t] = gated[t]
    sums_out[...] = jnp.broadcast_to(square_sums(gated)[None], sums_out.shape)


def last_kernel(sums, gated, gain, channels, out):
    steps, slots, width = gated.shape
    scale = row_scales(sums[...], channels, steps * slots)
    for t in range(steps):
        out[t] = (scaled(gated[t], scale[t * slots:(t + 1) * slots]) * gain[...]).astype(BF16)


def body(ssm_state, conv_window, x_in, z_gate, dt_raw, b_in, c_in, conv_weight, a_log, dt_bias, skip_d, norm_gain, parent):
    _, slots, heads, head_dim, nstate = ssm_state.shape
    steps, _, width = x_in.shape
    taps = conv_window.shape[2]
    rows = heads * head_dim
    tp = lax.axis_size("tp")
    pipes = lax.axis_size("pipe")
    count = lax.axis_size("roll")
    channels = width * tp
    npairs = len(pairs(steps))
    state = ssm_state.reshape(slots, rows, nstate)
    window = jnp.transpose(conv_window[0], (1, 0, 2))
    raw = jnp.transpose(dt_raw[0], (0, 2, 1))
    conv = conv_weight[0]
    shape = jax.ShapeDtypeStruct
    step_rows = shape((steps, slots, width), F32)
    packed_slot = shape((rows + 16, nstate), BF16)
    nextra = (2 * steps + npairs + taps + 4 + 7) // 8 * 8

    def at(i, p, t):
        return (i * pipes + p) * tp + t

    end = count - 1
    first_moves, second_moves = [], []
    for t in range(tp):
        first_moves += [(at(i, 0, t), at(i + 1, 1, t)) for i in range(end)]
        first_moves += [(at(i + 1, 1, t), at(i, 0, t)) for i in range(end)]
        first_moves += [(at(end, 0, t), at(end, 0, t ^ 1)), (at(0, 1, t), at(0, 1, t ^ 1))]
        second_moves += [(at(i, 1, t), at(i + 1, 1, t)) for i in range(end)]
        second_moves += [(at(i + 1, 0, t), at(i, 0, t)) for i in range(end)]
        second_moves += [(at(end, 1, t), at(end, 0, t)), (at(0, 0, t), at(0, 1, t))]
    swap = [(i, (i + 1) % pipes) for i in range(pipes)]

    leaving = pl.pallas_call(
        crossing_kernel,
        out_shape=packed_slot,
        in_specs=[HBM, HBM, HBM],
        out_specs=VMEM,
        scratch_shapes=[
            pltpu.SMEM(parent.shape, jnp.int32),
            pltpu.VMEM(window.shape, BF16),
            pltpu.SemaphoreType.DMA((3,)),
        ],
        compiler_params=PARAMS,
        name="crossing",
    )(*[pltpu.with_memory_space_constraint(value, pltpu.HBM) for value in (parent, state, window)])
    arrived = lax.ppermute(leaving, ("roll", "pipe", "tp"), first_moves)

    base, reach, mix, conv_part, cmask, wmask, leaving = pl.pallas_call(
        local_kernel,
        out_shape=(
            step_rows,
            step_rows,
            shape((npairs, slots, width), F32),
            shape((taps, slots, width), F32),
            shape((steps * slots, nstate), BF16),
            shape((slots, 128), F32),
            packed_slot,
        ),
        in_specs=[HBM, SMEM] + [VMEM] * 10,
        out_specs=(VMEM,) * 7,
        compiler_params=PARAMS,
        cost_estimate=pl.CostEstimate(flops=20_000_000, bytes_accessed=4_000_000, transcendentals=0),
        name="local",
    )(leaving, parent, state, window, c_in[0], b_in[0], raw, z_gate[0], conv, a_log, dt_bias, skip_d)

    pack, extra, row = pl.pallas_call(
        front_kernel,
        out_shape=(shape((steps * slots, width), F32), shape((nextra, width), F32), shape((8, 128), F32)),
        in_specs=[VMEM] * 9,
        out_specs=(VMEM,) * 3,
        compiler_params=PARAMS,
        name="front",
    )(base, reach, mix, conv_part, cmask, wmask, conv, x_in, norm_gain)
    other_extra = lax.ppermute(extra, "pipe", swap)
    other_pack = lax.ppermute(pack, "pipe", swap)
    later = lax.ppermute(leaving, ("roll", "pipe", "tp"), second_moves)

    whole, sums = pl.pallas_call(
        lambda *refs: fill_kernel(*refs[:5], taps, *refs[5:]),
        out_shape=(step_rows, shape((tp, 1, 128), F32)),
        in_specs=[VMEM] * 5,
        out_specs=(VMEM,) * 2,
        compiler_params=PARAMS,
        name="fill",
    )(arrived, other_pack, other_extra, row, wmask)
    section = lax.axis_index("pipe")
    sums = lax.cond(section == 0, lambda sums: sums, lambda sums: lax.all_to_all(sums, "tp", 0, 0), sums)
    rows_out = shape((steps, slots, width), BF16)
    norm, gated, sums = pl.pallas_call(
        lambda *refs: second_kernel(*refs[:10], channels, *refs[10:]),
        out_shape=(rows_out, step_rows, shape((tp, 1, 128), F32)),
        in_specs=[VMEM] * 10,
        out_specs=(VMEM,) * 3,
        compiler_params=PARAMS,
        name="second",
    )(sums, whole, later, base, reach, mix, conv_part, cmask, wmask, conv)
    other_norm = lax.ppermute(norm, "pipe", swap)

    def second_section(idle, sums, gated, gain):
        sums = lax.all_to_all(sums, "tp", 0, 0)
        return pl.pallas_call(
            lambda sums, gated, gain, out: last_kernel(sums, gated, gain, channels, out),
            out_shape=rows_out,
            in_specs=[VMEM] * 3,
            out_specs=VMEM,
            compiler_params=PARAMS,
            name="last",
        )(sums, gated, gain)

    result = lax.cond(section == 0, lambda idle, *others: idle, second_section, x_in, sums, gated, norm_gain)
    result = lax.cond(section == 0, lambda mine, sent: sent, lambda mine, sent: mine, result, other_norm)
    return result[None]


def solution(mesh):
    in_specs = (
        P("pipe", "roll", "tp", None, None),
        P("pipe", "roll", None, "tp"),
        P(None, "roll", "tp"),
        P("pipe", None, "roll", "tp"),
        P("pipe", None, "roll", "tp"),
        P("pipe", None, "roll", None),
        P("pipe", None, "roll", None),
        P("pipe", None, "tp"),
        P("pipe", "tp"),
        P("pipe", "tp"),
        P("pipe", "tp"),
        P("pipe", "tp"),
        P(),
    )
    out_specs = P("pipe", None, "roll", "tp")
    return jax.shard_map(body, mesh=mesh, in_specs=in_specs, out_specs=out_specs, check_vma=False)
```

```python
import jax
import jax.numpy as jnp
from jax import lax
from jax.experimental import pallas as pl
from jax.experimental.pallas import tpu as pltpu
from jax.sharding import PartitionSpec as P

F32 = jnp.float32
BF16 = jnp.bfloat16
VMEM = pl.BlockSpec(memory_space=pltpu.VMEM)
SMEM = pl.BlockSpec(memory_space=pltpu.SMEM)
HBM = pl.BlockSpec(memory_space=pltpu.HBM)
NT = (((1,), (1,)), ((), ()))
EPS = 1e-05
PARAMS = pltpu.CompilerParams(vmem_limit_bytes=24 * 1024 * 1024)


def silu(value):
    return value / (1.0 + jnp.exp(-value))


def tap_rows(conv):
    rows = conv[...].astype(F32)
    return [rows[k:k + 1] for k in range(rows.shape[0])]


def pairs(steps):
    return [(t, r) for t in range(steps) for r in range(t + 1)]


def crossing_row(parent, block, slots):
    begin = block * slots
    row = jnp.int32(0)
    for s in range(slots):
        found = parent[begin + s] - begin + slots
        row = jnp.where(found < slots, found, row)
    return jnp.clip(row, 0, slots - 1)


def packed_window(window, row):
    taps, slots, width = window.shape
    groups = width // 128
    pick = lax.broadcasted_iota(jnp.int32, (slots, 1), 0) == row
    place = lax.broadcasted_iota(jnp.int32, (16, 128), 0)
    packed = jnp.zeros(place.shape, F32)
    for k in range(taps):
        chosen = jnp.sum(jnp.where(pick, window[k].astype(F32), 0.0), axis=0, keepdims=True)
        for j in range(groups):
            packed = jnp.where(place == k * groups + j, chosen[:, j * 128:(j + 1) * 128], packed)
    return packed.astype(BF16)


def crossing_kernel(parent_hbm, state, window_hbm, out, parent, window, sems):
    slots = window.shape[1]
    nrows = state.shape[1]
    following = lax.axis_index("roll") + 1
    sends = (following < lax.axis_size("roll")) & (lax.axis_index("pipe") == 0)

    @pl.when(jnp.logical_not(sends))
    def _():
        out[...] = jnp.zeros(out.shape, BF16)

    @pl.when(sends)
    def _():
        get_parent = pltpu.make_async_copy(parent_hbm, parent, sems.at[0])
        get_parent.start()
        get_window = pltpu.make_async_copy(window_hbm, window, sems.at[1])
        get_window.start()
        get_parent.wait()
        row = crossing_row(parent, following, slots)
        copy = pltpu.make_async_copy(state.at[row], out.at[pl.ds(0, nrows)], sems.at[2])
        copy.start()
        get_window.wait()
        out[pl.ds(nrows, 16)] = packed_window(window, row)
        pad = out.shape[0] - nrows - 16
        out[pl.ds(nrows + 16, pad)] = jnp.zeros((pad, out.shape[1]), BF16)
        copy.wait()


def local_kernel(
    after, parent, state, window, c_in, b_in, dt_raw, z_gate, conv, a_log, dt_bias, skip_d,
    base_out, reach_out, mix_out, conv_out, cmask_out, wmask_out, leaving_out,
):
    steps, slots, width = z_gate.shape
    heads = dt_raw.shape[1]
    taps = window.shape[0]
    nstate = c_in.shape[2]
    roll = lax.axis_index("roll")
    first = roll * slots
    local = [parent[first + s] - first for s in range(slots)]
    held = [jnp.clip(row, 0, slots - 1) for row in local]

    slot_col = lax.broadcasted_iota(jnp.int32, (slots, slots), 0)
    slot_row = lax.broadcasted_iota(jnp.int32, (slots, slots), 1)
    choose = jnp.zeros((slots, slots), F32)
    slot_lane = lax.broadcasted_iota(jnp.int32, (slots, 128), 0)
    inside = jnp.zeros((slots, 128), F32)
    for s in range(slots):
        choose = jnp.where((slot_col == s) & (slot_row == local[s]), 1.0, choose)
        inside = jnp.where((slot_lane == s) & (local[s] >= 0), 1.0, inside)
    outside = 1.0 - inside
    wmask_out[...] = outside
    choose = choose.astype(BF16)

    taken = [jnp.dot(choose, window[k], preferred_element_type=F32) for k in range(taps)]
    weight = tap_rows(conv)
    for t in range(taps):
        part = weight[0] * taken[t]
        for k in range(1, taps - t):
            part = part + weight[k] * taken[t + k]
        conv_out[t] = part

    rate = jnp.exp(a_log[...])
    delta, decay = [], []
    for t in range(steps):
        raw = jnp.transpose(dt_raw[t]) + dt_bias[...]
        delta.append(jnp.maximum(raw, 0.0) + jnp.log1p(jnp.exp(-jnp.abs(raw))))
        decay.append(jnp.exp(-delta[t] * rate))
    c_rows = [c_in[t].astype(F32) for t in range(steps)]
    b_rows = [b_in[t].astype(F32) for t in range(steps)]
    coefs = []
    running = None
    for t in range(steps):
        running = decay[t] if running is None else running * decay[t]
        coefs.append(running)
    for t, r in pairs(steps):
        dot = jnp.sum(c_rows[t] * b_rows[r], axis=1, keepdims=True)
        coef = delta[r] * dot
        for j in range(r + 1, t + 1):
            coef = coef * decay[j]
        if t == r:
            coef = coef + skip_d[...]
        coefs.append(coef)
    stacked = jnp.concatenate(coefs, axis=0)
    head = lax.broadcasted_iota(jnp.int32, (heads, width), 0)
    lane_head = lax.broadcasted_iota(jnp.int32, (heads, width), 1) // (width // heads)
    expand = jnp.where(head == lane_head, 1.0, 0.0).astype(BF16)
    high = stacked.astype(BF16)
    low = (stacked - high.astype(F32)).astype(BF16)
    spread = jnp.dot(high, expand, preferred_element_type=F32) + jnp.dot(low, expand, preferred_element_type=F32)
    gate = [silu(z_gate[t].astype(F32)) for t in range(steps)]
    reach = []
    for t in range(steps):
        reach.append(spread[t * slots:(t + 1) * slots] * gate[t])
        reach_out[t] = reach[t]
    for i, (t, _) in enumerate(pairs(steps)):
        mix_out[i] = spread[(steps + i) * slots:(steps + i + 1) * slots] * gate[t]

    c_all = jnp.concatenate(c_rows, axis=0)
    slot_of = lax.rem(lax.broadcasted_iota(jnp.int32, (steps * slots, nstate), 0), slots)
    all_outside = jnp.concatenate([outside] * steps, axis=0)
    all_inside = 1.0 - all_outside
    cmask_out[...] = (c_all * all_outside).astype(BF16)
    c_inside = c_all * all_inside
    total = None
    for s in range(0, slots, 2):
        lhs = jnp.concatenate(
            [jnp.where(slot_of == s + i, c_inside, 0.0).astype(BF16) for i in range(2)], axis=1
        )
        rhs = jnp.concatenate([state[held[s]], state[held[s + 1]]], axis=1)
        part = lax.dot_general(lhs, rhs, NT, preferred_element_type=F32)
        total = part if total is None else total + part
    for t in range(steps):
        base_out[t] = total[t * slots:(t + 1) * slots] * reach[t]

    row = crossing_row(parent, lax.rem(roll + 1, lax.axis_size("roll")), slots)
    nrows = state.shape[1]
    leaving_out[pl.ds(0, nrows)] = state[row]
    leaving_out[pl.ds(nrows, 16)] = packed_window(window, row)


def gated_rows(pre, base, mix, steps):
    inner = [silu(value) for value in pre]
    rows = list(base)
    for i, (t, r) in enumerate(pairs(steps)):
        rows[t] = rows[t] + mix[i] * inner[r]
    return rows


def square_sums(rows):
    squares = []
    for row in rows:
        sq = row * row
        part = sq[:, :128]
        for j in range(1, sq.shape[1] // 128):
            part = part + sq[:, j * 128:(j + 1) * 128]
        squares.append(part)
    flat = jnp.concatenate(squares, axis=0)
    flat = jnp.concatenate([flat, jnp.zeros((128 - flat.shape[0], 128), F32)], axis=0)
    return jnp.sum(jnp.transpose(flat), axis=0, keepdims=True)


def row_scales(parts, channels, rows):
    totals = jnp.sum(parts, axis=0)[:1]
    scale = lax.rsqrt(totals * (1.0 / channels) + EPS)
    return jnp.transpose(jnp.broadcast_to(scale, (128, 128)))[:rows]


def scaled(row, scale):
    return jnp.concatenate(
        [row[:, j * 128:(j + 1) * 128] * scale for j in range(row.shape[1] // 128)], axis=1
    )


def with_inputs(window_part, weight, x_rows):
    taps = len(window_part)
    pre = []
    for t in range(len(x_rows)):
        part = window_part[t] if t < taps else None
        for k in range(max(0, taps - t), taps + 1):
            term = weight[k] * x_rows[t + k - taps]
            part = term if part is None else part + term
        pre.append(part)
    return pre


def arrived_rows(arrived, nrows, taps, groups):
    packed = arrived[pl.ds(nrows, 16)].astype(F32)
    rows = [
        jnp.concatenate([packed[k * groups + j:k * groups + j + 1] for j in range(groups)], axis=1)
        for k in range(taps)
    ]
    return arrived[pl.ds(0, nrows)], rows


def window_terms(weight, rows):
    taps = len(rows)
    parts = []
    for t in range(taps):
        part = weight[0] * rows[t]
        for k in range(1, taps - t):
            part = part + weight[k] * rows[t + k]
        parts.append(part)
    return parts


def front_kernel(base, reach, mix, conv_part, cmask, wmask, conv, x_in, gain, pack_out, extra_out, row_out):
    steps, slots, width = x_in.shape
    taps = conv_part.shape[0]
    lane = lax.broadcasted_iota(jnp.int32, (slots, 128), 1)
    slot = lax.broadcasted_iota(jnp.int32, (slots, 128), 0)
    lanes = jnp.sum(jnp.where(lax.rem(lane, slots) == slot, wmask[...], 0.0), axis=0, keepdims=True)
    row_out[...] = jnp.broadcast_to(lanes, row_out.shape)

    @pl.when(lax.axis_index("pipe") > 0)
    def _():
        pack_out[...] = jnp.zeros(pack_out.shape, F32)
        extra_out[...] = jnp.zeros(extra_out.shape, F32)

    @pl.when(lax.axis_index("pipe") == 0)
    def _():
        outside = wmask[:, :1]
        weight = tap_rows(conv)
        pre = with_inputs([conv_part[t] for t in range(taps)], weight, [x_in[t].astype(F32) for t in range(steps)])
        count = mix.shape[0]
        mixes = [mix[i] for i in range(count)]
        gated = gated_rows(pre, [base[t] for t in range(steps)], mixes, steps)
        gated = [row * (1.0 - outside) for row in gated]
        for t in range(steps):
            pack_out[pl.ds(t * slots, slots)] = gated[t] * gain[...]

        def crossing(value):
            return jnp.sum(value * outside, axis=0, keepdims=True)

        slot_c = [jnp.sum(cmask[pl.ds(t * slots, slots)].astype(F32), axis=0, keepdims=True) for t in range(steps)]
        rows = [crossing(reach[t]) for t in range(steps)]
        rows += [crossing(value) for value in mixes]
        rows += [crossing(value) for value in pre]
        rows += weight + [gain[...], jnp.concatenate(slot_c, axis=1)]
        sums = jnp.concatenate([square_sums(gated), jnp.zeros((1, width - 128), F32)], axis=1)
        pack_out[pl.ds(steps * slots, 8)] = jnp.concatenate([sums, jnp.zeros((7, width), F32)], axis=0)
        extra_out[...] = jnp.concatenate(rows + [jnp.zeros_like(gain)] * (extra_out.shape[0] - len(rows)), axis=0)


def fill_kernel(arrived, pack, extra, row, wmask, taps, other_out, sums_out):
    steps, slots, width = other_out.shape
    number = len(pairs(steps))
    nstate = arrived.shape[1]
    extra = extra[...]

    def take(begin, size):
        return [extra[begin + i:begin + i + 1] for i in range(size)]

    reach = take(0, steps)
    mixes = take(steps, number)
    pre = take(steps + number, steps)
    weight = take(2 * steps + number, taps + 1)
    gain, slot_c = take(2 * steps + number + taps + 1, 2)
    state, rows = arrived_rows(arrived, width, taps, width // 128)
    lhs = [slot_c[:, t * nstate:(t + 1) * nstate] for t in range(steps)]
    lhs = jnp.concatenate(lhs + [jnp.zeros((16 - steps, nstate), F32)], axis=0).astype(BF16)
    start = lax.dot_general(lhs, state, NT, preferred_element_type=F32)
    for t, term in enumerate(window_terms(weight, rows)):
        pre[t] = pre[t] + term
    gated = gated_rows(pre, [start[t:t + 1] * reach[t] for t in range(steps)], mixes, steps)
    mask = wmask[:, :1]
    lane = lax.broadcasted_iota(jnp.int32, (1, 128), 1)
    sums = jnp.zeros((1, 128), F32)
    for t in range(steps):
        other_out[t] = pack[pl.ds(t * slots, slots)] + mask * (gated[t] * gain)
        square = jnp.sum(gated[t] * gated[t], axis=1, keepdims=True)
        here = (lane >= t * slots) & (lane < (t + 1) * slots)
        sums = jnp.where(here, square, sums)
    sums = pack[pl.ds(steps * slots, 8)][:1, :128] + sums * row[pl.ds(0, 1)]
    sums_out[...] = jnp.broadcast_to(sums[None], sums_out.shape)


def second_kernel(
    sums, other, arrived, base, reach, mix, conv_part, cmask, wmask, conv, channels, norm_out, gated_out, sums_out
):
    steps, slots, width = other.shape
    taps = conv_part.shape[0]
    weight = tap_rows(conv)
    state, rows = arrived_rows(arrived, width, taps, width // 128)
    extra = lax.dot_general(cmask[...], state, NT, preferred_element_type=F32)
    start = [base[t] + extra[t * slots:(t + 1) * slots] * reach[t] for t in range(steps)]
    mask = wmask[:, :1]
    pre = [conv_part[t] + mask * term for t, term in enumerate(window_terms(weight, rows))]
    scale = row_scales(sums[...], channels, steps * slots)
    inputs = []
    for t in range(steps):
        row = scaled(other[t], scale[t * slots:(t + 1) * slots]).astype(BF16)
        norm_out[t] = row
        inputs.append(row.astype(F32))
    pre = with_inputs(pre, weight, inputs)
    gated = gated_rows(pre, start, [mix[i] for i in range(mix.shape[0])], steps)
    for t in range(steps):
        gated_out[t] = gated[t]
    sums_out[...] = jnp.broadcast_to(square_sums(gated)[None], sums_out.shape)


def last_kernel(sums, gated, gain, channels, out):
    steps, slots, width = gated.shape
    scale = row_scales(sums[...], channels, steps * slots)
    for t in range(steps):
        out[t] = (scaled(gated[t], scale[t * slots:(t + 1) * slots]) * gain[...]).astype(BF16)


def body(ssm_state, conv_window, x_in, z_gate, dt_raw, b_in, c_in, conv_weight, a_log, dt_bias, skip_d, norm_gain, parent):
    _, slots, heads, head_dim, nstate = ssm_state.shape
    steps, _, width = x_in.shape
    taps = conv_window.shape[2]
    rows = heads * head_dim
    tp = lax.axis_size("tp")
    pipes = lax.axis_size("pipe")
    count = lax.axis_size("roll")
    channels = width * tp
    npairs = len(pairs(steps))
    state = ssm_state.reshape(slots, rows, nstate)
    window = jnp.transpose(conv_window[0], (1, 0, 2))
    raw = jnp.transpose(dt_raw[0], (0, 2, 1))
    conv = conv_weight[0]
    shape = jax.ShapeDtypeStruct
    step_rows = shape((steps, slots, width), F32)
    packed_slot = shape((rows + 16, nstate), BF16)
    nextra = steps * slots + 8

    def at(i, p, t):
        return (i * pipes + p) * tp + t

    end = count - 1
    first_moves, second_moves = [], []
    for t in range(tp):
        first_moves += [(at(i, 0, t), at(i + 1, 1, t)) for i in range(end)]
        first_moves += [(at(i + 1, 1, t), at(i, 0, t)) for i in range(end)]
        first_moves += [(at(end, 0, t), at(end, 0, t ^ 1)), (at(0, 1, t), at(0, 1, t ^ 1))]
        second_moves += [(at(i, 1, t), at(i + 1, 1, t)) for i in range(end)]
        second_moves += [(at(i + 1, 0, t), at(i, 0, t)) for i in range(end)]
        second_moves += [(at(end, 1, t), at(end, 0, t)), (at(0, 0, t), at(0, 1, t))]
    swap = [(i, (i + 1) % pipes) for i in range(pipes)]

    leaving = pl.pallas_call(
        crossing_kernel,
        out_shape=shape((rows + 80, nstate), BF16),
        in_specs=[HBM, HBM, HBM],
        out_specs=VMEM,
        scratch_shapes=[
            pltpu.SMEM(parent.shape, jnp.int32),
            pltpu.VMEM(window.shape, BF16),
            pltpu.SemaphoreType.DMA((3,)),
        ],
        compiler_params=PARAMS,
        name="crossing",
    )(*[pltpu.with_memory_space_constraint(value, pltpu.HBM) for value in (parent, state, window)])
    arrived = lax.ppermute(leaving, ("roll", "pipe", "tp"), first_moves)

    base, reach, mix, conv_part, cmask, wmask, leaving = pl.pallas_call(
        local_kernel,
        out_shape=(
            step_rows,
            step_rows,
            shape((npairs, slots, width), F32),
            shape((taps, slots, width), F32),
            shape((steps * slots, nstate), BF16),
            shape((slots, 128), F32),
            packed_slot,
        ),
        in_specs=[HBM, SMEM] + [VMEM] * 10,
        out_specs=(VMEM,) * 7,
        compiler_params=PARAMS,
        cost_estimate=pl.CostEstimate(flops=20_000_000, bytes_accessed=4_000_000, transcendentals=0),
        name="local",
    )(leaving, parent, state, window, c_in[0], b_in[0], raw, z_gate[0], conv, a_log, dt_bias, skip_d)

    pack, extra, row = pl.pallas_call(
        front_kernel,
        out_shape=(shape((steps * slots + 8, width), F32), shape((nextra, width), F32), shape((8, 128), F32)),
        in_specs=[VMEM] * 9,
        out_specs=(VMEM,) * 3,
        compiler_params=PARAMS,
        name="front",
    )(base, reach, mix, conv_part, cmask, wmask, conv, x_in, norm_gain)
    other_extra = lax.ppermute(extra, "pipe", swap)
    other_pack = lax.ppermute(pack, "pipe", swap)
    later = lax.ppermute(leaving, ("roll", "pipe", "tp"), second_moves)

    whole, sums = pl.pallas_call(
        lambda *refs: fill_kernel(*refs[:5], taps, *refs[5:]),
        out_shape=(step_rows, shape((tp, 1, 128), F32)),
        in_specs=[VMEM] * 5,
        out_specs=(VMEM,) * 2,
        compiler_params=PARAMS,
        name="fill",
    )(arrived, other_pack, other_extra, row, wmask)
    section = lax.axis_index("pipe")
    sums = lax.cond(section == 0, lambda sums: sums, lambda sums: lax.all_to_all(sums, "tp", 0, 0), sums)
    rows_out = shape((steps, slots, width), BF16)
    norm, gated, sums = pl.pallas_call(
        lambda *refs: second_kernel(*refs[:10], channels, *refs[10:]),
        out_shape=(rows_out, step_rows, shape((tp, 1, 128), F32)),
        in_specs=[VMEM] * 10,
        out_specs=(VMEM,) * 3,
        compiler_params=PARAMS,
        name="second",
    )(sums, whole, later, base, reach, mix, conv_part, cmask, wmask, conv)
    other_norm = lax.ppermute(norm, "pipe", swap)

    def second_section(idle, sums, gated, gain):
        sums = lax.all_to_all(sums, "tp", 0, 0)
        return pl.pallas_call(
            lambda sums, gated, gain, out: last_kernel(sums, gated, gain, channels, out),
            out_shape=rows_out,
            in_specs=[VMEM] * 3,
            out_specs=VMEM,
            compiler_params=PARAMS,
            name="last",
        )(sums, gated, gain)

    result = lax.cond(section == 0, lambda idle, *others: idle, second_section, x_in, sums, gated, norm_gain)
    result = lax.cond(section == 0, lambda mine, sent: sent, lambda mine, sent: mine, result, other_norm)
    return result[None]


def solution(mesh):
    in_specs = (
        P("pipe", "roll", "tp", None, None),
        P("pipe", "roll", None, "tp"),
        P(None, "roll", "tp"),
        P("pipe", None, "roll", "tp"),
        P("pipe", None, "roll", "tp"),
        P("pipe", None, "roll", None),
        P("pipe", None, "roll", None),
        P("pipe", None, "tp"),
        P("pipe", "tp"),
        P("pipe", "tp"),
        P("pipe", "tp"),
        P("pipe", "tp"),
        P(),
    )
    out_specs = P("pipe", None, "roll", "tp")
    return jax.shard_map(body, mesh=mesh, in_specs=in_specs, out_specs=out_specs, check_vma=False)
```

```python
import jax
import jax.numpy as jnp
from jax import lax
from jax.experimental import pallas as pl
from jax.experimental.pallas import tpu as pltpu
from jax.sharding import PartitionSpec as P

F32 = jnp.float32
BF16 = jnp.bfloat16
VMEM = pl.BlockSpec(memory_space=pltpu.VMEM)
SMEM = pl.BlockSpec(memory_space=pltpu.SMEM)
HBM = pl.BlockSpec(memory_space=pltpu.HBM)
NT = (((1,), (1,)), ((), ()))
EPS = 1e-05
PARAMS = pltpu.CompilerParams(vmem_limit_bytes=24 * 1024 * 1024)


def silu(value):
    return value / (1.0 + jnp.exp(-value))


def tap_rows(conv):
    rows = conv[...].astype(F32)
    return [rows[k:k + 1] for k in range(rows.shape[0])]


def pairs(steps):
    return [(t, r) for t in range(steps) for r in range(t + 1)]


def crossing_row(parent, block, slots):
    begin = block * slots
    row = jnp.int32(0)
    for s in range(slots):
        found = parent[begin + s] - begin + slots
        row = jnp.where(found < slots, found, row)
    return jnp.clip(row, 0, slots - 1)


def packed_window(window, row):
    taps, slots, width = window.shape
    groups = width // 128
    pick = lax.broadcasted_iota(jnp.int32, (slots, 1), 0) == row
    place = lax.broadcasted_iota(jnp.int32, (16, 128), 0)
    packed = jnp.zeros(place.shape, F32)
    for k in range(taps):
        chosen = jnp.sum(jnp.where(pick, window[k].astype(F32), 0.0), axis=0, keepdims=True)
        for j in range(groups):
            packed = jnp.where(place == k * groups + j, chosen[:, j * 128:(j + 1) * 128], packed)
    return packed.astype(BF16)


def crossing_kernel(parent_hbm, state, window_hbm, out, parent, window, sems):
    slots = window.shape[1]
    nrows = state.shape[1]
    following = lax.axis_index("roll") + 1
    sends = (following < lax.axis_size("roll")) & (lax.axis_index("pipe") == 0)

    @pl.when(jnp.logical_not(sends))
    def _():
        out[...] = jnp.zeros(out.shape, BF16)

    @pl.when(sends)
    def _():
        get_parent = pltpu.make_async_copy(parent_hbm, parent, sems.at[0])
        get_parent.start()
        get_window = pltpu.make_async_copy(window_hbm, window, sems.at[1])
        get_window.start()
        get_parent.wait()
        row = crossing_row(parent, following, slots)
        copy = pltpu.make_async_copy(state.at[row], out.at[pl.ds(0, nrows)], sems.at[2])
        copy.start()
        get_window.wait()
        out[pl.ds(nrows, 16)] = packed_window(window, row)
        pad = out.shape[0] - nrows - 16
        out[pl.ds(nrows + 16, pad)] = jnp.zeros((pad, out.shape[1]), BF16)
        copy.wait()


def local_kernel(
    after, parent, state, window, c_in, b_in, dt_raw, z_gate, conv, a_log, dt_bias, skip_d,
    base_out, reach_out, mix_out, conv_out, cmask_out, wmask_out, leaving_out,
):
    steps, slots, width = z_gate.shape
    heads = dt_raw.shape[1]
    taps = window.shape[0]
    nstate = c_in.shape[2]
    roll = lax.axis_index("roll")
    first = roll * slots
    local = [parent[first + s] - first for s in range(slots)]
    held = [jnp.clip(row, 0, slots - 1) for row in local]

    slot_col = lax.broadcasted_iota(jnp.int32, (slots, slots), 0)
    slot_row = lax.broadcasted_iota(jnp.int32, (slots, slots), 1)
    choose = jnp.zeros((slots, slots), F32)
    slot_lane = lax.broadcasted_iota(jnp.int32, (slots, 128), 0)
    inside = jnp.zeros((slots, 128), F32)
    for s in range(slots):
        choose = jnp.where((slot_col == s) & (slot_row == local[s]), 1.0, choose)
        inside = jnp.where((slot_lane == s) & (local[s] >= 0), 1.0, inside)
    outside = 1.0 - inside
    wmask_out[...] = outside
    choose = choose.astype(BF16)

    taken = [jnp.dot(choose, window[k], preferred_element_type=F32) for k in range(taps)]
    weight = tap_rows(conv)
    for t in range(taps):
        part = weight[0] * taken[t]
        for k in range(1, taps - t):
            part = part + weight[k] * taken[t + k]
        conv_out[t] = part

    rate = jnp.exp(a_log[...])
    delta, decay = [], []
    for t in range(steps):
        raw = jnp.transpose(dt_raw[t]) + dt_bias[...]
        delta.append(jnp.maximum(raw, 0.0) + jnp.log1p(jnp.exp(-jnp.abs(raw))))
        decay.append(jnp.exp(-delta[t] * rate))
    c_rows = [c_in[t].astype(F32) for t in range(steps)]
    b_rows = [b_in[t].astype(F32) for t in range(steps)]
    coefs = []
    running = None
    for t in range(steps):
        running = decay[t] if running is None else running * decay[t]
        coefs.append(running)
    for t, r in pairs(steps):
        dot = jnp.sum(c_rows[t] * b_rows[r], axis=1, keepdims=True)
        coef = delta[r] * dot
        for j in range(r + 1, t + 1):
            coef = coef * decay[j]
        if t == r:
            coef = coef + skip_d[...]
        coefs.append(coef)
    stacked = jnp.concatenate(coefs, axis=0)
    head = lax.broadcasted_iota(jnp.int32, (heads, width), 0)
    lane_head = lax.broadcasted_iota(jnp.int32, (heads, width), 1) // (width // heads)
    expand = jnp.where(head == lane_head, 1.0, 0.0).astype(BF16)
    high = stacked.astype(BF16)
    low = (stacked - high.astype(F32)).astype(BF16)
    spread = jnp.dot(high, expand, preferred_element_type=F32) + jnp.dot(low, expand, preferred_element_type=F32)
    gate = [silu(z_gate[t].astype(F32)) for t in range(steps)]
    reach = []
    for t in range(steps):
        reach.append(spread[t * slots:(t + 1) * slots] * gate[t])
        reach_out[t] = reach[t]
    for i, (t, _) in enumerate(pairs(steps)):
        mix_out[i] = spread[(steps + i) * slots:(steps + i + 1) * slots] * gate[t]

    c_all = jnp.concatenate(c_rows, axis=0)
    slot_of = lax.rem(lax.broadcasted_iota(jnp.int32, (steps * slots, nstate), 0), slots)
    all_outside = jnp.concatenate([outside] * steps, axis=0)
    all_inside = 1.0 - all_outside
    cmask_out[...] = (c_all * all_outside).astype(BF16)
    c_inside = c_all * all_inside
    total = None
    for s in range(0, slots, 4):
        lhs = jnp.concatenate(
            [jnp.where(slot_of == s + i, c_inside, 0.0).astype(BF16) for i in range(4)], axis=1
        )
        rhs = jnp.concatenate([state[held[s + i]] for i in range(4)], axis=1)
        part = lax.dot_general(lhs, rhs, NT, preferred_element_type=F32)
        total = part if total is None else total + part
    for t in range(steps):
        base_out[t] = total[t * slots:(t + 1) * slots] * reach[t]

    row = crossing_row(parent, lax.rem(roll + 1, lax.axis_size("roll")), slots)
    nrows = state.shape[1]
    leaving_out[pl.ds(0, nrows)] = state[row]
    leaving_out[pl.ds(nrows, 16)] = packed_window(window, row)


def gated_rows(pre, base, mix, steps):
    inner = [silu(value) for value in pre]
    rows = list(base)
    for i, (t, r) in enumerate(pairs(steps)):
        rows[t] = rows[t] + mix[i] * inner[r]
    return rows


def square_sums(rows):
    squares = []
    for row in rows:
        sq = row * row
        part = sq[:, :128]
        for j in range(1, sq.shape[1] // 128):
            part = part + sq[:, j * 128:(j + 1) * 128]
        squares.append(part)
    flat = jnp.concatenate(squares, axis=0)
    flat = jnp.concatenate([flat, jnp.zeros((128 - flat.shape[0], 128), F32)], axis=0)
    return jnp.sum(jnp.transpose(flat), axis=0, keepdims=True)


def row_scales(parts, channels, rows):
    totals = jnp.sum(parts, axis=0)[:1]
    scale = lax.rsqrt(totals * (1.0 / channels) + EPS)
    return jnp.transpose(jnp.broadcast_to(scale, (128, 128)))[:rows]


def scaled(row, scale):
    return jnp.concatenate(
        [row[:, j * 128:(j + 1) * 128] * scale for j in range(row.shape[1] // 128)], axis=1
    )


def with_inputs(window_part, weight, x_rows):
    taps = len(window_part)
    pre = []
    for t in range(len(x_rows)):
        part = window_part[t] if t < taps else None
        for k in range(max(0, taps - t), taps + 1):
            term = weight[k] * x_rows[t + k - taps]
            part = term if part is None else part + term
        pre.append(part)
    return pre


def arrived_rows(arrived, nrows, taps, groups):
    packed = arrived[pl.ds(nrows, 16)].astype(F32)
    rows = [
        jnp.concatenate([packed[k * groups + j:k * groups + j + 1] for j in range(groups)], axis=1)
        for k in range(taps)
    ]
    return arrived[pl.ds(0, nrows)], rows


def window_terms(weight, rows):
    taps = len(rows)
    parts = []
    for t in range(taps):
        part = weight[0] * rows[t]
        for k in range(1, taps - t):
            part = part + weight[k] * rows[t + k]
        parts.append(part)
    return parts


def front_kernel(base, reach, mix, conv_part, cmask, wmask, conv, x_in, gain, pack_out, extra_out, row_out):
    steps, slots, width = x_in.shape
    taps = conv_part.shape[0]
    lane = lax.broadcasted_iota(jnp.int32, (slots, 128), 1)
    slot = lax.broadcasted_iota(jnp.int32, (slots, 128), 0)
    lanes = jnp.sum(jnp.where(lax.rem(lane, slots) == slot, wmask[...], 0.0), axis=0, keepdims=True)
    row_out[...] = jnp.broadcast_to(lanes, row_out.shape)

    @pl.when(lax.axis_index("pipe") > 0)
    def _():
        pack_out[...] = jnp.zeros(pack_out.shape, F32)
        extra_out[...] = jnp.zeros(extra_out.shape, F32)

    @pl.when(lax.axis_index("pipe") == 0)
    def _():
        outside = wmask[:, :1]
        weight = tap_rows(conv)
        pre = with_inputs([conv_part[t] for t in range(taps)], weight, [x_in[t].astype(F32) for t in range(steps)])
        count = mix.shape[0]
        mixes = [mix[i] for i in range(count)]
        gated = gated_rows(pre, [base[t] for t in range(steps)], mixes, steps)
        gated = [row * (1.0 - outside) for row in gated]
        for t in range(steps):
            pack_out[pl.ds(t * slots, slots)] = gated[t] * gain[...]

        def crossing(value):
            return jnp.sum(value * outside, axis=0, keepdims=True)

        slot_c = [jnp.sum(cmask[pl.ds(t * slots, slots)].astype(F32), axis=0, keepdims=True) for t in range(steps)]
        rows = [crossing(reach[t]) for t in range(steps)]
        rows += [crossing(value) for value in mixes]
        rows += [crossing(value) for value in pre]
        rows += weight + [gain[...], jnp.concatenate(slot_c, axis=1)]
        sums = jnp.concatenate([square_sums(gated), jnp.zeros((1, width - 128), F32)], axis=1)
        pack_out[pl.ds(steps * slots, 8)] = jnp.concatenate([sums, jnp.zeros((7, width), F32)], axis=0)
        extra_out[...] = jnp.concatenate(rows + [jnp.zeros_like(gain)] * (extra_out.shape[0] - len(rows)), axis=0)


def fill_kernel(arrived, pack, extra, row, wmask, taps, other_out, sums_out):
    steps, slots, width = other_out.shape
    number = len(pairs(steps))
    nstate = arrived.shape[1]
    extra = extra[...]

    def take(begin, size):
        return [extra[begin + i:begin + i + 1] for i in range(size)]

    reach = take(0, steps)
    mixes = take(steps, number)
    pre = take(steps + number, steps)
    weight = take(2 * steps + number, taps + 1)
    gain, slot_c = take(2 * steps + number + taps + 1, 2)
    state, rows = arrived_rows(arrived, width, taps, width // 128)
    lhs = [slot_c[:, t * nstate:(t + 1) * nstate] for t in range(steps)]
    lhs = jnp.concatenate(lhs + [jnp.zeros((16 - steps, nstate), F32)], axis=0).astype(BF16)
    start = lax.dot_general(lhs, state, NT, preferred_element_type=F32)
    for t, term in enumerate(window_terms(weight, rows)):
        pre[t] = pre[t] + term
    gated = gated_rows(pre, [start[t:t + 1] * reach[t] for t in range(steps)], mixes, steps)
    mask = wmask[:, :1]
    lane = lax.broadcasted_iota(jnp.int32, (1, 128), 1)
    sums = jnp.zeros((1, 128), F32)
    for t in range(steps):
        other_out[t] = pack[pl.ds(t * slots, slots)] + mask * (gated[t] * gain)
        square = jnp.sum(gated[t] * gated[t], axis=1, keepdims=True)
        here = (lane >= t * slots) & (lane < (t + 1) * slots)
        sums = jnp.where(here, square, sums)
    sums = pack[pl.ds(steps * slots, 8)][:1, :128] + sums * row[pl.ds(0, 1)]
    sums_out[...] = jnp.broadcast_to(sums[None], sums_out.shape)


def second_kernel(
    sums, other, arrived, base, reach, mix, conv_part, cmask, wmask, conv, channels, norm_out, gated_out, sums_out
):
    steps, slots, width = other.shape
    taps = conv_part.shape[0]
    weight = tap_rows(conv)
    state, rows = arrived_rows(arrived, width, taps, width // 128)
    extra = lax.dot_general(cmask[...], state, NT, preferred_element_type=F32)
    start = [base[t] + extra[t * slots:(t + 1) * slots] * reach[t] for t in range(steps)]
    mask = wmask[:, :1]
    pre = [conv_part[t] + mask * term for t, term in enumerate(window_terms(weight, rows))]
    scale = row_scales(sums[...], channels, steps * slots)
    inputs = []
    for t in range(steps):
        row = scaled(other[t], scale[t * slots:(t + 1) * slots]).astype(BF16)
        norm_out[t] = row
        inputs.append(row.astype(F32))
    pre = with_inputs(pre, weight, inputs)
    gated = gated_rows(pre, start, [mix[i] for i in range(mix.shape[0])], steps)
    for t in range(steps):
        gated_out[t] = gated[t]
    sums_out[...] = jnp.broadcast_to(square_sums(gated)[None], sums_out.shape)


def last_kernel(sums, gated, gain, channels, out):
    steps, slots, width = gated.shape
    scale = row_scales(sums[...], channels, steps * slots)
    for t in range(steps):
        out[t] = (scaled(gated[t], scale[t * slots:(t + 1) * slots]) * gain[...]).astype(BF16)


def body(ssm_state, conv_window, x_in, z_gate, dt_raw, b_in, c_in, conv_weight, a_log, dt_bias, skip_d, norm_gain, parent):
    _, slots, heads, head_dim, nstate = ssm_state.shape
    steps, _, width = x_in.shape
    taps = conv_window.shape[2]
    rows = heads * head_dim
    tp = lax.axis_size("tp")
    pipes = lax.axis_size("pipe")
    count = lax.axis_size("roll")
    channels = width * tp
    npairs = len(pairs(steps))
    state = ssm_state.reshape(slots, rows, nstate)
    window = jnp.transpose(conv_window[0], (1, 0, 2))
    raw = jnp.transpose(dt_raw[0], (0, 2, 1))
    conv = conv_weight[0]
    shape = jax.ShapeDtypeStruct
    step_rows = shape((steps, slots, width), F32)
    packed_slot = shape((rows + 16, nstate), BF16)
    nextra = steps * slots + 8

    def at(i, p, t):
        return (i * pipes + p) * tp + t

    end = count - 1
    first_moves, second_moves = [], []
    for t in range(tp):
        first_moves += [(at(i, 0, t), at(i + 1, 1, t)) for i in range(end)]
        first_moves += [(at(i + 1, 1, t), at(i, 0, t)) for i in range(end)]
        first_moves += [(at(end, 0, t), at(end, 0, t ^ 1)), (at(0, 1, t), at(0, 1, t ^ 1))]
        second_moves += [(at(i, 1, t), at(i + 1, 1, t)) for i in range(end)]
        second_moves += [(at(i + 1, 0, t), at(i, 0, t)) for i in range(end)]
        second_moves += [(at(end, 1, t), at(end, 0, t)), (at(0, 0, t), at(0, 1, t))]
    swap = [(i, (i + 1) % pipes) for i in range(pipes)]

    leaving = pl.pallas_call(
        crossing_kernel,
        out_shape=shape((rows + 80, nstate), BF16),
        in_specs=[HBM, HBM, HBM],
        out_specs=VMEM,
        scratch_shapes=[
            pltpu.SMEM(parent.shape, jnp.int32),
            pltpu.VMEM(window.shape, BF16),
            pltpu.SemaphoreType.DMA((3,)),
        ],
        compiler_params=PARAMS,
        name="crossing",
    )(*[pltpu.with_memory_space_constraint(value, pltpu.HBM) for value in (parent, state, window)])
    arrived = lax.ppermute(leaving, ("roll", "pipe", "tp"), first_moves)

    base, reach, mix, conv_part, cmask, wmask, leaving = pl.pallas_call(
        local_kernel,
        out_shape=(
            step_rows,
            step_rows,
            shape((npairs, slots, width), F32),
            shape((taps, slots, width), F32),
            shape((steps * slots, nstate), BF16),
            shape((slots, 128), F32),
            packed_slot,
        ),
        in_specs=[HBM, SMEM] + [VMEM] * 10,
        out_specs=(VMEM,) * 7,
        compiler_params=PARAMS,
        cost_estimate=pl.CostEstimate(flops=20_000_000, bytes_accessed=4_000_000, transcendentals=0),
        name="local",
    )(leaving, parent, state, window, c_in[0], b_in[0], raw, z_gate[0], conv, a_log, dt_bias, skip_d)

    pack, extra, row = pl.pallas_call(
        front_kernel,
        out_shape=(shape((steps * slots + 8, width), F32), shape((nextra, width), F32), shape((8, 128), F32)),
        in_specs=[VMEM] * 9,
        out_specs=(VMEM,) * 3,
        compiler_params=PARAMS,
        name="front",
    )(base, reach, mix, conv_part, cmask, wmask, conv, x_in, norm_gain)
    other_extra = lax.ppermute(extra, "pipe", swap)
    other_pack = lax.ppermute(pack, "pipe", swap)
    later = lax.ppermute(leaving, ("roll", "pipe", "tp"), second_moves)

    whole, sums = pl.pallas_call(
        lambda *refs: fill_kernel(*refs[:5], taps, *refs[5:]),
        out_shape=(step_rows, shape((tp, 1, 128), F32)),
        in_specs=[VMEM] * 5,
        out_specs=(VMEM,) * 2,
        compiler_params=PARAMS,
        name="fill",
    )(arrived, other_pack, other_extra, row, wmask)
    section = lax.axis_index("pipe")
    sums = lax.cond(section == 0, lambda sums: sums, lambda sums: lax.all_to_all(sums, "tp", 0, 0), sums)
    rows_out = shape((steps, slots, width), BF16)
    norm, gated, sums = pl.pallas_call(
        lambda *refs: second_kernel(*refs[:10], channels, *refs[10:]),
        out_shape=(rows_out, step_rows, shape((tp, 1, 128), F32)),
        in_specs=[VMEM] * 10,
        out_specs=(VMEM,) * 3,
        compiler_params=PARAMS,
        name="second",
    )(sums, whole, later, base, reach, mix, conv_part, cmask, wmask, conv)
    other_norm = lax.ppermute(norm, "pipe", swap)

    def second_section(idle, sums, gated, gain):
        sums = lax.all_to_all(sums, "tp", 0, 0)
        return pl.pallas_call(
            lambda sums, gated, gain, out: last_kernel(sums, gated, gain, channels, out),
            out_shape=rows_out,
            in_specs=[VMEM] * 3,
            out_specs=VMEM,
            compiler_params=PARAMS,
            name="last",
        )(sums, gated, gain)

    result = lax.cond(section == 0, lambda idle, *others: idle, second_section, x_in, sums, gated, norm_gain)
    result = lax.cond(section == 0, lambda mine, sent: sent, lambda mine, sent: mine, result, other_norm)
    return result[None]


def solution(mesh):
    in_specs = (
        P("pipe", "roll", "tp", None, None),
        P("pipe", "roll", None, "tp"),
        P(None, "roll", "tp"),
        P("pipe", None, "roll", "tp"),
        P("pipe", None, "roll", "tp"),
        P("pipe", None, "roll", None),
        P("pipe", None, "roll", None),
        P("pipe", None, "tp"),
        P("pipe", "tp"),
        P("pipe", "tp"),
        P("pipe", "tp"),
        P("pipe", "tp"),
        P(),
    )
    out_specs = P("pipe", None, "roll", "tp")
    return jax.shard_map(body, mesh=mesh, in_specs=in_specs, out_specs=out_specs, check_vma=False)
```

```python
import jax
import jax.numpy as jnp
from jax import lax
from jax.experimental import pallas as pl
from jax.experimental.pallas import tpu as pltpu
from jax.sharding import PartitionSpec as P

F32 = jnp.float32
BF16 = jnp.bfloat16
VMEM = pl.BlockSpec(memory_space=pltpu.VMEM)
SMEM = pl.BlockSpec(memory_space=pltpu.SMEM)
HBM = pl.BlockSpec(memory_space=pltpu.HBM)
NT = (((1,), (1,)), ((), ()))
EPS = 1e-05
PARAMS = pltpu.CompilerParams(vmem_limit_bytes=24 * 1024 * 1024)


def silu(value):
    half = 0.5 * value
    return half + half * jnp.tanh(half)


def tap_rows(conv):
    rows = conv[...].astype(F32)
    return [rows[k:k + 1] for k in range(rows.shape[0])]


def pairs(steps):
    return [(t, r) for t in range(steps) for r in range(t + 1)]


def crossing_row(parent, block, slots):
    begin = block * slots
    row = jnp.int32(0)
    for s in range(slots):
        found = parent[begin + s] - begin + slots
        row = jnp.where(found < slots, found, row)
    return jnp.clip(row, 0, slots - 1)


def packed_window(window, row):
    taps, slots, width = window.shape
    groups = width // 128
    pick = lax.broadcasted_iota(jnp.int32, (slots, 1), 0) == row
    place = lax.broadcasted_iota(jnp.int32, (16, 128), 0)
    packed = jnp.zeros(place.shape, F32)
    for k in range(taps):
        chosen = jnp.sum(jnp.where(pick, window[k].astype(F32), 0.0), axis=0, keepdims=True)
        for j in range(groups):
            packed = jnp.where(place == k * groups + j, chosen[:, j * 128:(j + 1) * 128], packed)
    return packed.astype(BF16)


def crossing_kernel(parent_hbm, state, window_hbm, out, parent, window, sems):
    slots = window.shape[1]
    nrows = state.shape[1]
    following = lax.axis_index("roll") + 1
    sends = (following < lax.axis_size("roll")) & (lax.axis_index("pipe") == 0)

    @pl.when(jnp.logical_not(sends))
    def _():
        out[...] = jnp.zeros(out.shape, BF16)

    @pl.when(sends)
    def _():
        get_parent = pltpu.make_async_copy(parent_hbm, parent, sems.at[0])
        get_parent.start()
        get_window = pltpu.make_async_copy(window_hbm, window, sems.at[1])
        get_window.start()
        get_parent.wait()
        row = crossing_row(parent, following, slots)
        copy = pltpu.make_async_copy(state.at[row], out.at[pl.ds(0, nrows)], sems.at[2])
        copy.start()
        get_window.wait()
        out[pl.ds(nrows, 16)] = packed_window(window, row)
        pad = out.shape[0] - nrows - 16
        out[pl.ds(nrows + 16, pad)] = jnp.zeros((pad, out.shape[1]), BF16)
        copy.wait()


def local_kernel(
    after, parent, state, window, c_in, b_in, dt_raw, z_gate, conv, a_log, dt_bias, skip_d,
    base_out, reach_out, mix_out, conv_out, cmask_out, wmask_out, leaving_out,
):
    steps, slots, width = z_gate.shape
    heads = dt_raw.shape[1]
    taps = window.shape[0]
    nstate = c_in.shape[2]
    roll = lax.axis_index("roll")
    first = roll * slots
    local = [parent[first + s] - first for s in range(slots)]
    held = [jnp.clip(row, 0, slots - 1) for row in local]

    slot_col = lax.broadcasted_iota(jnp.int32, (slots, slots), 0)
    slot_row = lax.broadcasted_iota(jnp.int32, (slots, slots), 1)
    choose = jnp.zeros((slots, slots), F32)
    slot_lane = lax.broadcasted_iota(jnp.int32, (slots, 128), 0)
    inside = jnp.zeros((slots, 128), F32)
    for s in range(slots):
        choose = jnp.where((slot_col == s) & (slot_row == local[s]), 1.0, choose)
        inside = jnp.where((slot_lane == s) & (local[s] >= 0), 1.0, inside)
    outside = 1.0 - inside
    wmask_out[...] = outside
    choose = choose.astype(BF16)

    taken = [jnp.dot(choose, window[k], preferred_element_type=F32) for k in range(taps)]
    weight = tap_rows(conv)
    for t in range(taps):
        part = weight[0] * taken[t]
        for k in range(1, taps - t):
            part = part + weight[k] * taken[t + k]
        conv_out[t] = part

    rate = jnp.exp(a_log[...])
    delta, decay = [], []
    for t in range(steps):
        raw = jnp.transpose(dt_raw[t]) + dt_bias[...]
        delta.append(jnp.maximum(raw, 0.0) + jnp.log1p(jnp.exp(-jnp.abs(raw))))
        decay.append(jnp.exp(-delta[t] * rate))
    c_rows = [c_in[t].astype(F32) for t in range(steps)]
    b_rows = [b_in[t].astype(F32) for t in range(steps)]
    coefs = []
    running = None
    for t in range(steps):
        running = decay[t] if running is None else running * decay[t]
        coefs.append(running)
    for t, r in pairs(steps):
        dot = jnp.sum(c_rows[t] * b_rows[r], axis=1, keepdims=True)
        coef = delta[r] * dot
        for j in range(r + 1, t + 1):
            coef = coef * decay[j]
        if t == r:
            coef = coef + skip_d[...]
        coefs.append(coef)
    stacked = jnp.concatenate(coefs, axis=0)
    head = lax.broadcasted_iota(jnp.int32, (heads, width), 0)
    lane_head = lax.broadcasted_iota(jnp.int32, (heads, width), 1) // (width // heads)
    expand = jnp.where(head == lane_head, 1.0, 0.0).astype(BF16)
    high = stacked.astype(BF16)
    low = (stacked - high.astype(F32)).astype(BF16)
    spread = jnp.dot(high, expand, preferred_element_type=F32) + jnp.dot(low, expand, preferred_element_type=F32)
    gate = [silu(z_gate[t].astype(F32)) for t in range(steps)]
    reach = []
    for t in range(steps):
        reach.append(spread[t * slots:(t + 1) * slots] * gate[t])
        reach_out[t] = reach[t]
    for i, (t, _) in enumerate(pairs(steps)):
        mix_out[i] = spread[(steps + i) * slots:(steps + i + 1) * slots] * gate[t]

    c_all = jnp.concatenate(c_rows, axis=0)
    slot_of = lax.rem(lax.broadcasted_iota(jnp.int32, (steps * slots, nstate), 0), slots)
    all_outside = jnp.concatenate([outside] * steps, axis=0)
    all_inside = 1.0 - all_outside
    cmask_out[...] = (c_all * all_outside).astype(BF16)
    c_inside = c_all * all_inside
    total = None
    for s in range(0, slots, 4):
        lhs = jnp.concatenate(
            [jnp.where(slot_of == s + i, c_inside, 0.0).astype(BF16) for i in range(4)], axis=1
        )
        rhs = jnp.concatenate([state[held[s + i]] for i in range(4)], axis=1)
        part = lax.dot_general(lhs, rhs, NT, preferred_element_type=F32)
        total = part if total is None else total + part
    for t in range(steps):
        base_out[t] = total[t * slots:(t + 1) * slots] * reach[t]

    row = crossing_row(parent, lax.rem(roll + 1, lax.axis_size("roll")), slots)
    nrows = state.shape[1]
    leaving_out[pl.ds(0, nrows)] = state[row]
    leaving_out[pl.ds(nrows, 16)] = packed_window(window, row)


def gated_rows(pre, base, mix, steps):
    inner = [silu(value) for value in pre]
    rows = list(base)
    for i, (t, r) in enumerate(pairs(steps)):
        rows[t] = rows[t] + mix[i] * inner[r]
    return rows


def square_sums(rows):
    squares = []
    for row in rows:
        sq = row * row
        part = sq[:, :128]
        for j in range(1, sq.shape[1] // 128):
            part = part + sq[:, j * 128:(j + 1) * 128]
        squares.append(part)
    flat = jnp.concatenate(squares, axis=0)
    flat = jnp.concatenate([flat, jnp.zeros((128 - flat.shape[0], 128), F32)], axis=0)
    return jnp.sum(jnp.transpose(flat), axis=0, keepdims=True)


def row_scales(parts, channels, rows):
    totals = jnp.sum(parts, axis=0)[:1]
    scale = lax.rsqrt(totals * (1.0 / channels) + EPS)
    return jnp.transpose(jnp.broadcast_to(scale, (128, 128)))[:rows]


def scaled(row, scale):
    return jnp.concatenate(
        [row[:, j * 128:(j + 1) * 128] * scale for j in range(row.shape[1] // 128)], axis=1
    )


def with_inputs(window_part, weight, x_rows):
    taps = len(window_part)
    pre = []
    for t in range(len(x_rows)):
        part = window_part[t] if t < taps else None
        for k in range(max(0, taps - t), taps + 1):
            term = weight[k] * x_rows[t + k - taps]
            part = term if part is None else part + term
        pre.append(part)
    return pre


def arrived_rows(arrived, nrows, taps, groups):
    packed = arrived[pl.ds(nrows, 16)].astype(F32)
    rows = [
        jnp.concatenate([packed[k * groups + j:k * groups + j + 1] for j in range(groups)], axis=1)
        for k in range(taps)
    ]
    return arrived[pl.ds(0, nrows)], rows


def window_terms(weight, rows):
    taps = len(rows)
    parts = []
    for t in range(taps):
        part = weight[0] * rows[t]
        for k in range(1, taps - t):
            part = part + weight[k] * rows[t + k]
        parts.append(part)
    return parts


def front_kernel(base, reach, mix, conv_part, cmask, wmask, conv, x_in, gain, pack_out, extra_out, row_out):
    steps, slots, width = x_in.shape
    taps = conv_part.shape[0]
    lane = lax.broadcasted_iota(jnp.int32, (slots, 128), 1)
    slot = lax.broadcasted_iota(jnp.int32, (slots, 128), 0)
    lanes = jnp.sum(jnp.where(lax.rem(lane, slots) == slot, wmask[...], 0.0), axis=0, keepdims=True)
    row_out[...] = jnp.broadcast_to(lanes, row_out.shape)

    @pl.when(lax.axis_index("pipe") > 0)
    def _():
        pack_out[...] = jnp.zeros(pack_out.shape, F32)
        extra_out[...] = jnp.zeros(extra_out.shape, F32)

    @pl.when(lax.axis_index("pipe") == 0)
    def _():
        outside = wmask[:, :1]
        weight = tap_rows(conv)
        pre = with_inputs([conv_part[t] for t in range(taps)], weight, [x_in[t].astype(F32) for t in range(steps)])
        count = mix.shape[0]
        mixes = [mix[i] for i in range(count)]
        gated = gated_rows(pre, [base[t] for t in range(steps)], mixes, steps)
        gated = [row * (1.0 - outside) for row in gated]
        for t in range(steps):
            pack_out[pl.ds(t * slots, slots)] = gated[t] * gain[...]

        def crossing(value):
            return jnp.sum(value * outside, axis=0, keepdims=True)

        slot_c = [jnp.sum(cmask[pl.ds(t * slots, slots)].astype(F32), axis=0, keepdims=True) for t in range(steps)]
        rows = [crossing(reach[t]) for t in range(steps)]
        rows += [crossing(value) for value in mixes]
        rows += [crossing(value) for value in pre]
        rows += weight + [gain[...], jnp.concatenate(slot_c, axis=1)]
        sums = jnp.concatenate([square_sums(gated), jnp.zeros((1, width - 128), F32)], axis=1)
        pack_out[pl.ds(steps * slots, 8)] = jnp.concatenate([sums, jnp.zeros((7, width), F32)], axis=0)
        extra_out[...] = jnp.concatenate(rows + [jnp.zeros_like(gain)] * (extra_out.shape[0] - len(rows)), axis=0)


def fill_kernel(arrived, pack, extra, row, wmask, taps, other_out, sums_out):
    steps, slots, width = other_out.shape
    number = len(pairs(steps))
    nstate = arrived.shape[1]
    extra = extra[...]

    def take(begin, size):
        return [extra[begin + i:begin + i + 1] for i in range(size)]

    reach = take(0, steps)
    mixes = take(steps, number)
    pre = take(steps + number, steps)
    weight = take(2 * steps + number, taps + 1)
    gain, slot_c = take(2 * steps + number + taps + 1, 2)
    state, rows = arrived_rows(arrived, width, taps, width // 128)
    lhs = [slot_c[:, t * nstate:(t + 1) * nstate] for t in range(steps)]
    lhs = jnp.concatenate(lhs + [jnp.zeros((16 - steps, nstate), F32)], axis=0).astype(BF16)
    start = lax.dot_general(lhs, state, NT, preferred_element_type=F32)
    for t, term in enumerate(window_terms(weight, rows)):
        pre[t] = pre[t] + term
    gated = gated_rows(pre, [start[t:t + 1] * reach[t] for t in range(steps)], mixes, steps)
    mask = wmask[:, :1]
    lane = lax.broadcasted_iota(jnp.int32, (1, 128), 1)
    sums = jnp.zeros((1, 128), F32)
    for t in range(steps):
        other_out[t] = pack[pl.ds(t * slots, slots)] + mask * (gated[t] * gain)
        square = jnp.sum(gated[t] * gated[t], axis=1, keepdims=True)
        here = (lane >= t * slots) & (lane < (t + 1) * slots)
        sums = jnp.where(here, square, sums)
    sums = pack[pl.ds(steps * slots, 8)][:1, :128] + sums * row[pl.ds(0, 1)]
    sums_out[...] = jnp.broadcast_to(sums[None], sums_out.shape)


def second_kernel(
    sums, other, arrived, base, reach, mix, conv_part, cmask, wmask, conv, channels, norm_out, gated_out, sums_out
):
    steps, slots, width = other.shape
    taps = conv_part.shape[0]
    weight = tap_rows(conv)
    state, rows = arrived_rows(arrived, width, taps, width // 128)
    extra = lax.dot_general(cmask[...], state, NT, preferred_element_type=F32)
    start = [base[t] + extra[t * slots:(t + 1) * slots] * reach[t] for t in range(steps)]
    mask = wmask[:, :1]
    pre = [conv_part[t] + mask * term for t, term in enumerate(window_terms(weight, rows))]
    scale = row_scales(sums[...], channels, steps * slots)
    inputs = []
    for t in range(steps):
        row = scaled(other[t], scale[t * slots:(t + 1) * slots]).astype(BF16)
        norm_out[t] = row
        inputs.append(row.astype(F32))
    pre = with_inputs(pre, weight, inputs)
    gated = gated_rows(pre, start, [mix[i] for i in range(mix.shape[0])], steps)
    for t in range(steps):
        gated_out[t] = gated[t]
    sums_out[...] = jnp.broadcast_to(square_sums(gated)[None], sums_out.shape)


def last_kernel(sums, gated, gain, channels, out):
    steps, slots, width = gated.shape
    scale = row_scales(sums[...], channels, steps * slots)
    for t in range(steps):
        out[t] = (scaled(gated[t], scale[t * slots:(t + 1) * slots]) * gain[...]).astype(BF16)


def body(ssm_state, conv_window, x_in, z_gate, dt_raw, b_in, c_in, conv_weight, a_log, dt_bias, skip_d, norm_gain, parent):
    _, slots, heads, head_dim, nstate = ssm_state.shape
    steps, _, width = x_in.shape
    taps = conv_window.shape[2]
    rows = heads * head_dim
    tp = lax.axis_size("tp")
    pipes = lax.axis_size("pipe")
    count = lax.axis_size("roll")
    channels = width * tp
    npairs = len(pairs(steps))
    state = ssm_state.reshape(slots, rows, nstate)
    window = jnp.transpose(conv_window[0], (1, 0, 2))
    raw = jnp.transpose(dt_raw[0], (0, 2, 1))
    conv = conv_weight[0]
    shape = jax.ShapeDtypeStruct
    step_rows = shape((steps, slots, width), F32)
    packed_slot = shape((rows + 16, nstate), BF16)
    nextra = steps * slots + 8

    def at(i, p, t):
        return (i * pipes + p) * tp + t

    end = count - 1
    first_moves, second_moves = [], []
    for t in range(tp):
        first_moves += [(at(i, 0, t), at(i + 1, 1, t)) for i in range(end)]
        first_moves += [(at(i + 1, 1, t), at(i, 0, t)) for i in range(end)]
        first_moves += [(at(end, 0, t), at(end, 0, t ^ 1)), (at(0, 1, t), at(0, 1, t ^ 1))]
        second_moves += [(at(i, 1, t), at(i + 1, 1, t)) for i in range(end)]
        second_moves += [(at(i + 1, 0, t), at(i, 0, t)) for i in range(end)]
        second_moves += [(at(end, 1, t), at(end, 0, t)), (at(0, 0, t), at(0, 1, t))]
    swap = [(i, (i + 1) % pipes) for i in range(pipes)]

    leaving = pl.pallas_call(
        crossing_kernel,
        out_shape=shape((rows + 80, nstate), BF16),
        in_specs=[HBM, HBM, HBM],
        out_specs=VMEM,
        scratch_shapes=[
            pltpu.SMEM(parent.shape, jnp.int32),
            pltpu.VMEM(window.shape, BF16),
            pltpu.SemaphoreType.DMA((3,)),
        ],
        compiler_params=PARAMS,
        name="crossing",
    )(*[pltpu.with_memory_space_constraint(value, pltpu.HBM) for value in (parent, state, window)])
    arrived = lax.ppermute(leaving, ("roll", "pipe", "tp"), first_moves)

    base, reach, mix, conv_part, cmask, wmask, leaving = pl.pallas_call(
        local_kernel,
        out_shape=(
            step_rows,
            step_rows,
            shape((npairs, slots, width), F32),
            shape((taps, slots, width), F32),
            shape((steps * slots, nstate), BF16),
            shape((slots, 128), F32),
            packed_slot,
        ),
        in_specs=[HBM, SMEM] + [VMEM] * 10,
        out_specs=(VMEM,) * 7,
        compiler_params=PARAMS,
        cost_estimate=pl.CostEstimate(flops=20_000_000, bytes_accessed=4_000_000, transcendentals=0),
        name="local",
    )(leaving, parent, state, window, c_in[0], b_in[0], raw, z_gate[0], conv, a_log, dt_bias, skip_d)

    pack, extra, row = pl.pallas_call(
        front_kernel,
        out_shape=(shape((steps * slots + 8, width), F32), shape((nextra, width), F32), shape((8, 128), F32)),
        in_specs=[VMEM] * 9,
        out_specs=(VMEM,) * 3,
        compiler_params=PARAMS,
        name="front",
    )(base, reach, mix, conv_part, cmask, wmask, conv, x_in, norm_gain)
    other_extra = lax.ppermute(extra, "pipe", swap)
    other_pack = lax.ppermute(pack, "pipe", swap)
    later = lax.ppermute(leaving, ("roll", "pipe", "tp"), second_moves)

    whole, sums = pl.pallas_call(
        lambda *refs: fill_kernel(*refs[:5], taps, *refs[5:]),
        out_shape=(step_rows, shape((tp, 1, 128), F32)),
        in_specs=[VMEM] * 5,
        out_specs=(VMEM,) * 2,
        compiler_params=PARAMS,
        name="fill",
    )(arrived, other_pack, other_extra, row, wmask)
    section = lax.axis_index("pipe")
    sums = lax.cond(section == 0, lambda sums: sums, lambda sums: lax.all_to_all(sums, "tp", 0, 0), sums)
    rows_out = shape((steps, slots, width), BF16)
    norm, gated, sums = pl.pallas_call(
        lambda *refs: second_kernel(*refs[:10], channels, *refs[10:]),
        out_shape=(rows_out, step_rows, shape((tp, 1, 128), F32)),
        in_specs=[VMEM] * 10,
        out_specs=(VMEM,) * 3,
        compiler_params=PARAMS,
        name="second",
    )(sums, whole, later, base, reach, mix, conv_part, cmask, wmask, conv)
    other_norm = lax.ppermute(norm, "pipe", swap)

    def second_section(idle, sums, gated, gain):
        sums = lax.all_to_all(sums, "tp", 0, 0)
        return pl.pallas_call(
            lambda sums, gated, gain, out: last_kernel(sums, gated, gain, channels, out),
            out_shape=rows_out,
            in_specs=[VMEM] * 3,
            out_specs=VMEM,
            compiler_params=PARAMS,
            name="last",
        )(sums, gated, gain)

    result = lax.cond(section == 0, lambda idle, *others: idle, second_section, x_in, sums, gated, norm_gain)
    result = lax.cond(section == 0, lambda mine, sent: sent, lambda mine, sent: mine, result, other_norm)
    return result[None]


def solution(mesh):
    in_specs = (
        P("pipe", "roll", "tp", None, None),
        P("pipe", "roll", None, "tp"),
        P(None, "roll", "tp"),
        P("pipe", None, "roll", "tp"),
        P("pipe", None, "roll", "tp"),
        P("pipe", None, "roll", None),
        P("pipe", None, "roll", None),
        P("pipe", None, "tp"),
        P("pipe", "tp"),
        P("pipe", "tp"),
        P("pipe", "tp"),
        P("pipe", "tp"),
        P(),
    )
    out_specs = P("pipe", None, "roll", "tp")
    return jax.shard_map(body, mesh=mesh, in_specs=in_specs, out_specs=out_specs, check_vma=False)
```
